32 devices in a mesh: context: 8 (over y, x, core), tensor: 4 (over z).
Axes of the slice: x: 2, y: 2, z: 4, core: 2. Of those that a mesh axis runs over, the one named last changes fastest.
Arguments:
- tokens_t: bfloat16 [6144, 2048], P('tensor', 'context'), may hold values from -6 to 6
- qkv_weight: bfloat16 [6144, 24576], P(None, 'tensor'), may hold values from -1.5309311 to 1.5309311, as said below
- prior_state: float32 [64, 128, 128], P('tensor'), may hold values from -192 to 192
- norm_gain: float32 [8192], P('tensor'), may hold values from 0.1 to 1.9
Outputs:
- mixed: bfloat16 [2048, 8192], P('context', 'tensor')
The draws below stay inside these ranges and needn't reach their ends.
Inputs may be any that keep to these rules, and one draw needn't show every extreme that they name: `qkv_weight`: column h * 3 * 128 + p * 128 + e projects onto feature e of head h, with p = 0, 1, 2 for query, key and value.
All inputs are finite; a program needn't handle non-finite values.
Results may differ from the reference program's by a relative error of at most 0.0034.
Values may be sent and summed in bfloat16 or wider, within the bound.
No kernel may reach another device: no remote copies, remote signals or barrier semaphores. Data moves between devices by JAX's collectives and lax.ppermute only.
A program may use at most 128 MiB of HBM per device.

```python
import jax
import jax.numpy as jnp
from jax import lax

D = 6144
H = 64
HEAD = 128
GROUP = 256
TOKENS = 2048
N_CONTEXT = 8


def draw_qkv_weight(key, part):
    base = jnp.clip(jax.random.normal(key, (D, H, 3, HEAD), jnp.float32), -6.0, 6.0)
    head_pos = jnp.arange(H, dtype=jnp.float32) / max(H - 1, 1)
    top_scale = 10.0
    value_scale = top_scale ** head_pos
    part_scale = jnp.where(jnp.arange(3)[None, :] == 2, value_scale[:, None], 1.0)
    drawn = base * part_scale[None, :, :, None] * D ** (-0.5)
    return drawn.reshape(D, H * 3 * HEAD).astype(jnp.bfloat16)


def block_levels(key, extent, pieces, low, largest):
    def one(axis_at, shards_of):
        draws = jax.random.uniform(jax.random.fold_in(jax.random.fold_in(key, 6), axis_at), (shards_of,), jnp.float32, low / len(pieces), largest / len(pieces))
        return jnp.repeat(jnp.exp(draws), extent[axis_at] // shards_of).reshape((-1,) + (1,) * (len(extent) - axis_at - 1))

    gain = one(*pieces[0])
    for cut in pieces[1:]:
        gain = gain * one(*cut)
    return gain


def gaussian(stream_key, dims, spread, most, pieces=(), kind=jnp.bfloat16):
    result = spread * jax.random.normal(stream_key, dims, jnp.float32)
    if pieces:
        result = result * block_levels(stream_key, dims, pieces, -0.22, 0.18)
    return jnp.clip(result, -most, most).astype(kind)


def setup_inputs(seed: int = 0) -> dict:
    seeds = jax.random.split(jax.random.key(seed), 5)
    return {
        "tokens_t": gaussian(seeds[0], (D, TOKENS), 1.0, 6.0, ((0, 4), (1, 8))),
        "qkv_weight": draw_qkv_weight(jax.random.fold_in(seeds[4], 71), 0),
        "prior_state": gaussian(seeds[2], (H, HEAD, HEAD), (GROUP / 8), 192.0, ((0, 4),), jnp.float32),
        "norm_gain": jnp.clip(1.0 + 0.18 * jax.random.normal(seeds[3], (H * HEAD,), jnp.float32), 0.1, 1.9),
    }


EPSILON = 1e-06
PRECISE = lax.Precision.HIGHEST

def reference(tokens_t, qkv_weight, prior_state, norm_gain):
    features = tokens_t.T.astype(jnp.float32)
    stacked = qkv_weight.reshape(D, H, 3 * HEAD).transpose(1, 0, 2)
    causal = jnp.arange(GROUP)[:, None] >= jnp.arange(GROUP)[None, :]

    def one_head(operands):
        w_head, prior_kv = operands
        projected = jnp.dot(features, w_head.astype(jnp.float32), preferred_element_type=jnp.float32, precision=PRECISE)
        activated = lax.optimization_barrier(jax.nn.silu(projected).astype(jnp.bfloat16)).astype(jnp.float32)
        blocks = activated.reshape(N_CONTEXT, GROUP, 3, HEAD)
        queries = blocks[:, :, 0]
        key_rows = blocks[:, :, 1]
        value_rows = blocks[:, :, 2]
        states = jnp.einsum('ctd,cte->cde', key_rows, value_rows, precision=PRECISE)
        zero_state = jnp.zeros((1, HEAD, HEAD), jnp.float32)
        carried = prior_kv[None] + jnp.concatenate([zero_state, jnp.cumsum(states, axis=0)[:-1]], axis=0)
        scores = jnp.einsum('ctd,csd->cts', queries, key_rows, precision=PRECISE)
        scores = jnp.where(causal[None], scores, 0.0)
        scores = lax.optimization_barrier(scores.astype(jnp.bfloat16)).astype(jnp.float32)
        within = jnp.einsum('cts,csd->ctd', scores, value_rows, precision=PRECISE)
        across = jnp.einsum('ctd,cde->cte', queries, carried, precision=PRECISE)
        return (within + across).reshape(TOKENS, HEAD)
    attended = lax.map(one_head, (stacked, prior_state.astype(jnp.float32)))
    attended = attended.transpose(1, 0, 2).reshape(TOKENS, H * HEAD)
    mean_sq = lax.optimization_barrier(jnp.mean(attended * attended, axis=1, keepdims=True))
    return (attended * lax.rsqrt(mean_sq + EPSILON) * norm_gain[None, :]).astype(jnp.bfloat16)
```

```python
import functools

import jax
import jax.numpy as jnp
from jax import lax
from jax.experimental import pallas as pl
from jax.experimental.pallas import tpu as pltpu
from jax.sharding import PartitionSpec as P

EPSILON = 1e-06
PARTS = 3
CHUNKS = 2
COLUMNS = 1024
VMEM_LIMIT = 32 * 1024 * 1024

F32 = jnp.float32
BF16 = jnp.bfloat16


def params():
    return pltpu.CompilerParams(vmem_limit_bytes=VMEM_LIMIT)


WHOLE = pl.BlockSpec(memory_space=pltpu.VMEM)
ANY = pl.BlockSpec(memory_space=pl.ANY)


def feature_copies(pieces, raw, sems):
    rows = pieces[0].shape[0]
    return [
        pltpu.make_async_copy(piece, raw.at[pl.ds(j * rows, rows)], sems.at[j])
        for j, piece in enumerate(pieces)
    ]


def start_features(pick, choices, raw, sems):
    for c, pieces in enumerate(choices):

        @pl.when(pick == c)
        def _(pieces=pieces):
            for copy in feature_copies(pieces, raw, sems):
                copy.start()


def wait_features(choices, raw, sems):
    for copy in feature_copies(choices[0], raw, sems):
        copy.wait()


def column_blocks(columns):
    width = COLUMNS if columns % COLUMNS == 0 else columns
    return [pl.ds(at, width) for at in range(0, columns, width)]


def project_kernel(n_choices, n_pieces, first, ahead, info, *refs):
    count = n_choices * n_pieces
    choices = [refs[c * n_pieces : (c + 1) * n_pieces] for c in range(n_choices)]
    weight = refs[count]
    refs = refs[count + (1 if first else 2) :]
    total, refs = refs[0], refs[1:]
    if ahead:
        slab, refs = refs[0], refs[1:]
    raw, turned, held, sems, weight_sems = refs
    rows, columns = held.shape
    blocks = column_blocks(columns)

    start_features(info[0], choices, raw, sems)
    at = pl.ds(pl.multiple_of(info[1] * rows, rows), rows)
    copies = [
        pltpu.make_async_copy(weight.at[at, block], held.at[:, block], weight_sems.at[b])
        for b, block in enumerate(blocks)
    ]
    for copy in copies:
        copy.start()
    if ahead:
        later = pl.ds(pl.multiple_of(info[2] * ahead, ahead), ahead)
        slab_copy = pltpu.make_async_copy(
            weight.at[later, :], slab, weight_sems.at[len(blocks)]
        )
        slab_copy.start()
    wait_features(choices, raw, sems)
    turned[...] = raw[...].T
    for copy, block in zip(copies, blocks):
        copy.wait()
        product = jnp.dot(turned[...], held[:, block], preferred_element_type=F32)
        if first:
            total[:, block] = product
        else:
            total[:, block] += product
    if ahead:
        slab_copy.wait()


def project(choices, info, weight, total, ahead=0):
    n_choices, n_pieces = len(choices), len(choices[0])
    piece_rows, tokens = choices[0][0].shape
    rows, columns = piece_rows * n_pieces, weight.shape[1]
    first = total is None
    flat = [piece for pieces in choices for piece in pieces]
    operands = flat + [weight] + ([] if first else [total])
    out_shape = [pltpu.VMEM((tokens, columns), F32)]
    if ahead:
        out_shape.append(pltpu.VMEM((ahead, columns), BF16))
    out = pl.pallas_call(
        functools.partial(project_kernel, n_choices, n_pieces, first, ahead),
        out_shape=out_shape,
        in_specs=[pl.BlockSpec(memory_space=pltpu.SMEM)]
        + [ANY] * (len(flat) + 1)
        + ([] if first else [WHOLE]),
        out_specs=[WHOLE] * len(out_shape),
        scratch_shapes=[
            pltpu.VMEM((rows, tokens), BF16),
            pltpu.VMEM((tokens, rows), BF16),
            pltpu.VMEM((rows, columns), BF16),
            pltpu.SemaphoreType.DMA((n_pieces,)),
            pltpu.SemaphoreType.DMA((len(column_blocks(columns)) + 1,)),
        ],
        input_output_aliases={} if first else {len(operands): 0},
        compiler_params=params(),
        cost_estimate=pl.CostEstimate(
            flops=2 * tokens * rows * columns,
            bytes_accessed=(rows + ahead) * columns * 2 + rows * tokens * 2,
            transcendentals=0,
        ),
        name="project",
    )(info, *operands)
    return out if ahead else out[0]


def activate_kernel(n_choices, width, info, *refs):
    choices = [[ref] for ref in refs[:n_choices]]
    slab, total, act_ref, state_ref, raw, turned, sems = refs[n_choices:]
    heads = state_ref.shape[0]
    start_features(info[0], choices, raw, sems)
    wait_features(choices, raw, sems)
    turned[...] = raw[...].T
    group = PARTS * width
    for h in range(heads):
        block = pl.ds(h * group, group)
        projected = total[:, block] + jnp.dot(
            turned[...], slab[:, block], preferred_element_type=F32
        )
        act = (projected / (1.0 + jnp.exp(-projected))).astype(BF16)
        act_ref[:, block] = act
        state_ref[lax.rem(h + info[1], heads)] = lax.dot_general(
            act[:, width : 2 * width],
            act[:, 2 * width :],
            (((0,), (0,)), ((), ())),
            preferred_element_type=F32,
        )


def activate(choices, info, slab, total, width):
    tokens = choices[0].shape[1]
    rows, columns = slab.shape
    heads = columns // (PARTS * width)
    return pl.pallas_call(
        functools.partial(activate_kernel, len(choices), width),
        out_shape=(
            pltpu.VMEM((tokens, columns), BF16),
            jax.ShapeDtypeStruct((heads, width, width), F32),
        ),
        in_specs=[pl.BlockSpec(memory_space=pltpu.SMEM)] + [ANY] * len(choices) + [WHOLE] * 2,
        out_specs=(WHOLE, WHOLE),
        scratch_shapes=[
            pltpu.VMEM((rows, tokens), BF16),
            pltpu.VMEM((tokens, rows), BF16),
            pltpu.SemaphoreType.DMA((1,)),
        ],
        compiler_params=params(),
        cost_estimate=pl.CostEstimate(
            flops=2 * tokens * rows * columns + 2 * heads * tokens * width * width,
            bytes_accessed=rows * tokens * 2,
            transcendentals=tokens * columns,
        ),
        name="activate",
    )(info, *choices, slab, total)


def within_kernel(width, act_ref, within_ref):
    tokens, columns = act_ref.shape
    causal = lax.broadcasted_iota(jnp.int32, (tokens, tokens), 0) >= lax.broadcasted_iota(
        jnp.int32, (tokens, tokens), 1
    )
    for h in range(columns // (PARTS * width)):
        at = h * PARTS * width
        queries = act_ref[:, at : at + width]
        keys = act_ref[:, at + width : at + 2 * width]
        values = act_ref[:, at + 2 * width : at + 3 * width]
        scores = lax.dot_general(
            queries, keys, (((1,), (1,)), ((), ())), preferred_element_type=F32
        )
        scores = jnp.where(causal, scores, 0.0).astype(BF16)
        within_ref[:, h * width : (h + 1) * width] = jnp.dot(
            scores, values, preferred_element_type=F32
        )


def attend_within(act, width):
    tokens, columns = act.shape
    heads = columns // (PARTS * width)
    return pl.pallas_call(
        functools.partial(within_kernel, width),
        out_shape=pltpu.VMEM((tokens, heads * width), F32),
        in_specs=[WHOLE],
        out_specs=WHOLE,
        compiler_params=params(),
        cost_estimate=pl.CostEstimate(
            flops=4 * heads * tokens * tokens * width,
            bytes_accessed=tokens * columns * 2,
            transcendentals=0,
        ),
        name="within",
    )(act)


def across_kernel(info, act, within, prior, mine, other, att_ref, square_ref):
    width = prior.shape[1]
    half = mine.shape[0]
    squares = None
    for step in range(half):
        for side, earlier in ((info[0], mine), (1 - info[0], other)):
            head = side * half + step
            carried = prior[head] + earlier[step]
            upper = carried.astype(BF16)
            lower = (carried - upper.astype(F32)).astype(BF16)
            queries = act[:, pl.ds(pl.multiple_of(head * (PARTS * width), width), width)]
            columns = pl.ds(pl.multiple_of(head * width, width), width)
            attended = within[:, columns] + jnp.dot(
                jnp.concatenate([queries, queries], axis=1),
                jnp.concatenate([upper, lower], axis=0),
                preferred_element_type=F32,
            )
            att_ref[:, columns] = attended
            square = attended * attended
            squares = square if squares is None else squares + square
    square_ref[...] = lax.dot_general(
        jnp.ones((8, width), F32),
        squares,
        (((1,), (1,)), ((), ())),
        preferred_element_type=F32,
        precision=lax.Precision.HIGHEST,
    )


def attend_across(info, act, within, prior, mine, other):
    tokens = act.shape[0]
    heads, width, _ = prior.shape
    return pl.pallas_call(
        across_kernel,
        out_shape=(
            pltpu.VMEM((tokens, heads * width), F32),
            jax.ShapeDtypeStruct((8, tokens), F32),
        ),
        in_specs=[pl.BlockSpec(memory_space=pltpu.SMEM)] + [WHOLE] * 5,
        out_specs=(WHOLE, WHOLE),
        input_output_aliases={2: 0},
        compiler_params=params(),
        cost_estimate=pl.CostEstimate(
            flops=4 * heads * tokens * width * width, bytes_accessed=0, transcendentals=0
        ),
        name="across",
    )(info, act, within, prior, mine, other)


def norm_kernel(features, att_ref, square_ref, gain_ref, out_ref):
    ones = jnp.ones((square_ref.shape[0], 128), F32)
    mean_sq = lax.dot_general(
        square_ref[...] * (1.0 / square_ref.shape[0] / features),
        ones,
        (((0,), (0,)), ((), ())),
        preferred_element_type=F32,
        precision=lax.Precision.HIGHEST,
    )
    inverse = lax.rsqrt(mean_sq + EPSILON)
    for at in range(0, att_ref.shape[1], 128):
        out_ref[:, at : at + 128] = (
            att_ref[:, at : at + 128] * inverse * gain_ref[:, at : at + 128]
        ).astype(BF16)


def normalize(att, squares, gain, features):
    tokens, columns = att.shape
    return pl.pallas_call(
        functools.partial(norm_kernel, features),
        out_shape=jax.ShapeDtypeStruct((tokens, columns), BF16),
        in_specs=[WHOLE] * 3,
        out_specs=WHOLE,
        compiler_params=params(),
        cost_estimate=pl.CostEstimate(
            flops=2 * tokens * columns, bytes_accessed=2 * tokens * columns, transcendentals=0
        ),
        name="normalize",
    )(att, squares, gain[None, :])


def sum_over_tensor(x, n):
    if n & (n - 1):
        return lax.psum(x, "tensor")
    bit = 1
    while bit < n:
        x = x + lax.ppermute(x, "tensor", [(i, i ^ bit) for i in range(n)])
        bit *= 2
    return x


def earlier_states(states, n):
    half = states.shape[0] // 2
    index = lax.axis_index("context")
    core, chip, chips = index % 2, index // 2, n // 2
    swap = [(i, i ^ 1) for i in range(n)]
    own = states[half:]
    theirs = lax.ppermute(states[:half], "context", swap)
    total = own + theirs
    before = jnp.zeros_like(own)
    bit = 1
    while bit < chips:
        last = bit * 2 >= chips
        pairs = [
            (2 * i + c, 2 * (i ^ bit) + c)
            for i in range(chips)
            for c in range(2)
            if not (last and i & bit)
        ]
        arrived = lax.ppermute(total.astype(BF16), "context", pairs).astype(F32)
        before = before + (arrived if last else jnp.where(chip & bit, arrived, 0.0))
        total = total + arrived
        bit *= 2
    for_mate = before + jnp.where(core == 0, own, 0.0)
    mine = before + jnp.where(core == 1, theirs, 0.0)
    other = lax.ppermute(for_mate, "context", swap)
    return mine, other


def body(n_tensor, n_context, tokens_t, qkv_weight, prior_state, norm_gain):
    share = tokens_t.shape[0]
    heads, width, _ = prior_state.shape
    place = lax.axis_index("tensor")
    core = lax.axis_index("context") % 2

    piece = share // CHUNKS
    left = [[tokens_t[j * piece : (j + 1) * piece] for j in range(CHUNKS)]]
    right = [left[0]]
    for s in range(1, n_tensor):
        up = [(i, i + 1) for i in range(s - 1, n_tensor - 1)]
        down = [(i, i - 1) for i in range(1, n_tensor - s + 1)]
        left.append([])
        right.append([])
        for j in range(CHUNKS):
            left[s].append(lax.ppermute(left[s - 1][j], "tensor", up))
            right[s].append(lax.ppermute(right[s - 1][j], "tensor", down))

    def ints(*values):
        return jnp.stack([jnp.asarray(v, jnp.int32) for v in values])

    def source(m):
        return jnp.where(place >= m, place - m, m)

    last = n_tensor - 1
    piece_last = source(last) * CHUNKS + CHUNKS - 1
    total, slab = project(
        [[tokens_t]], ints(0, place, piece_last), qkv_weight, None, ahead=piece
    )
    for m in range(1, n_tensor):
        pick = jnp.where(place >= m, 0, m - place)
        choices = [left[m]] + [right[s] for s in range(1, m + 1)]
        if m < last:
            total = project(choices, ints(pick, source(m)), qkv_weight, total)
        else:
            for j in range(CHUNKS - 1):
                one = [[c[j]] for c in choices]
                total = project(one, ints(pick, source(m) * CHUNKS + j), qkv_weight, total)
            one = [c[CHUNKS - 1] for c in choices]
            shift = jnp.where(core == 0, heads // 2, 0)
            act, states = activate(one, ints(pick, shift), slab, total, width)
    mine, other = earlier_states(states, n_context)
    within = attend_within(act, width)
    att, squares = attend_across(ints(core), act, within, prior_state, mine, other)
    squares = sum_over_tensor(squares, n_tensor)
    return normalize(att, squares, norm_gain, n_tensor * heads * width)


def solution(mesh):
    n_tensor, n_context = mesh.shape["tensor"], mesh.shape["context"]
    in_specs = (P("tensor", "context"), P(None, "tensor"), P("tensor", None, None), P("tensor"))
    return jax.shard_map(
        functools.partial(body, n_tensor, n_context),
        mesh=mesh,
        in_specs=in_specs,
        out_specs=P("context", "tensor"),
        check_vma=False,
    )
```

```python
import functools

import jax
import jax.numpy as jnp
from jax import lax
from jax.experimental import pallas as pl
from jax.experimental.pallas import tpu as pltpu
from jax.sharding import PartitionSpec as P

EPSILON = 1e-06
PARTS = 3
COLUMNS = 1536
VMEM_EXTRA = 4 * 1024 * 1024

F32 = jnp.float32
BF16 = jnp.bfloat16


def params(scratch):
    return pltpu.CompilerParams(vmem_limit_bytes=scratch + VMEM_EXTRA)


HBM = pl.BlockSpec(memory_space=pltpu.HBM)
WHOLE = pl.BlockSpec(memory_space=pltpu.VMEM)
ANY = pl.BlockSpec(memory_space=pl.ANY)


def start_features(pick, choices, raw, sem):
    for c, pieces in enumerate(choices):

        @pl.when(pick == c)
        def _(pieces=pieces):
            at = 0
            for piece in pieces:
                there = raw.at[pl.ds(at, piece.shape[0])]
                pltpu.make_async_copy(piece, there, sem).start()
                at += piece.shape[0]


def wait_features(raw, sem):
    pltpu.make_async_copy(raw, raw, sem).wait()


def of_place(values):
    place = lax.axis_index("tensor")
    found = jnp.int32(values[0])
    for i, value in enumerate(values[1:], 1):
        if value != values[0]:
            found = jnp.where(place == i, jnp.int32(value), found)
    return found


def column_blocks(columns):
    width = COLUMNS if columns % COLUMNS == 0 else columns
    return [pl.ds(at, width) for at in range(0, columns, width)]


def project_kernel(counts, first, picks, weight_rows, *refs):
    refs = list(refs)
    choices = [[refs.pop(0) for _ in range(count)] for count in counts]
    weight = refs.pop(0)
    if not first:
        refs.pop(0)
    total, done, raw, turned, held, sem, weight_sems = refs
    done[...] = jnp.zeros_like(done)
    rows, columns = held.shape
    blocks = column_blocks(columns)

    start_features(of_place(picks), choices, raw, sem)
    at = pl.ds(pl.multiple_of(of_place(weight_rows), 16), rows)
    copies = [
        pltpu.make_async_copy(weight.at[at, block], held.at[:, block], weight_sems.at[b])
        for b, block in enumerate(blocks)
    ]
    for copy in copies:
        copy.start()
    wait_features(raw, sem)
    turned[...] = raw[...].T
    for copy, block in zip(copies, blocks):
        copy.wait()
        product = jnp.dot(turned[...], held[:, block], preferred_element_type=F32)
        if first:
            total[:, block] = product
        else:
            total[:, block] += product


def project(choices, picks, weight_rows, weight, total):
    counts = [len(pieces) for pieces in choices]
    rows = sum(piece.shape[0] for piece in choices[0])
    tokens, columns = choices[0][0].shape[1], weight.shape[1]
    first = total is None
    flat = [piece for pieces in choices for piece in pieces]
    operands = flat + [weight] + ([] if first else [total])
    return pl.pallas_call(
        functools.partial(project_kernel, counts, first, picks, weight_rows),
        out_shape=(pltpu.VMEM((tokens, columns), F32), pltpu.VMEM((8, 128), F32)),
        in_specs=[HBM if first else ANY] * len(flat) + [HBM] + ([] if first else [WHOLE]),
        out_specs=(WHOLE, WHOLE),
        scratch_shapes=[
            pltpu.VMEM((rows, tokens), BF16),
            pltpu.VMEM((tokens, rows), BF16),
            pltpu.VMEM((rows, columns), BF16),
            pltpu.SemaphoreType.DMA,
            pltpu.SemaphoreType.DMA((len(column_blocks(columns)),)),
        ],
        input_output_aliases={} if first else {len(operands) - 1: 0},
        compiler_params=params(2 * rows * (columns + 2 * tokens)),
        cost_estimate=pl.CostEstimate(
            flops=2 * tokens * rows * columns,
            bytes_accessed=rows * columns * 2 + rows * tokens * 2,
            transcendentals=0,
        ),
        name="project",
    )(*operands)


def heads_at_once(half):
    return next(g for g in (4, 2, 1) if half % g == 0)


def activate_heads(first_column, width, turned, held, total, act_ref, state_ref, arrived):
    half = state_ref.shape[0]
    group = PARTS * width
    at_once = heads_at_once(half)
    for h in range(0, half, at_once):
        arrived(h // at_once)
        here = slice(h * group, (h + at_once) * group)
        block = pl.ds(pl.multiple_of(first_column + h * group, group), at_once * group)
        projected = total[:, block] + jnp.dot(
            turned[...], held[:, here], preferred_element_type=F32
        )
        act = (projected / (1.0 + jnp.exp(-projected))).astype(BF16)
        act_ref[:, here] = act
        for g in range(at_once):
            at = g * group
            state_ref[h + g] = lax.dot_general(
                act[:, at + width : at + 2 * width],
                act[:, at + 2 * width : at + group],
                (((0,), (0,)), ((), ())),
                preferred_element_type=F32,
            )


def first_kernel(n_choices, width, picks, weight_rows, *refs):
    choices = [[ref] for ref in refs[:n_choices]]
    weight, total, turned, rest, act_ref, state_ref, raw, held, sem, weight_sems = refs[
        n_choices:
    ]
    rows, columns = held.shape
    block = heads_at_once(state_ref.shape[0]) * PARTS * width
    core = lax.axis_index("context") % 2
    start_features(of_place(picks), choices, raw, sem)
    at = pl.ds(pl.multiple_of(of_place(weight_rows), 16), rows)
    copies = []
    for b in range(columns // block):
        here = pl.ds(pl.multiple_of((1 - core) * columns + b * block, block), block)
        there = held.at[:, pl.ds(b * block, block)]
        copies.append(pltpu.make_async_copy(weight.at[at, here], there, weight_sems.at[b]))
    here = pl.ds(pl.multiple_of(core * columns, block), columns)
    rest_copy = pltpu.make_async_copy(weight.at[at, here], rest, weight_sems.at[len(copies)])
    for copy in copies:
        copy.start()
    rest_copy.start()
    wait_features(raw, sem)
    turned[...] = raw[...].T
    activate_heads(
        (1 - core) * columns,
        width,
        turned,
        held,
        total,
        act_ref,
        state_ref,
        lambda b: copies[b].wait(),
    )
    rest_copy.wait()


def second_kernel(width, turned, held, total, act_ref, state_ref):
    core = lax.axis_index("context") % 2
    activate_heads(
        core * held.shape[1], width, turned, held, total, act_ref, state_ref, lambda b: None
    )


def activate(choices, picks, weight_rows, weight, total, heads, width):
    rows, tokens = choices[0].shape
    half = heads // 2
    columns = half * PARTS * width
    blocks = half // heads_at_once(half)
    outs = (
        pltpu.VMEM((tokens, columns), BF16),
        pltpu.VMEM((half, width, width), F32),
    )
    cost = pl.CostEstimate(
        flops=2 * tokens * rows * columns + 2 * half * tokens * width * width,
        bytes_accessed=rows * tokens * 2,
        transcendentals=tokens * columns,
    )
    turned, rest, act_other, state_other = pl.pallas_call(
        functools.partial(first_kernel, len(choices), width, picks, weight_rows),
        out_shape=(pltpu.VMEM((tokens, rows), BF16), pltpu.VMEM((rows, columns), BF16)) + outs,
        in_specs=[ANY] * len(choices) + [HBM, WHOLE],
        out_specs=(WHOLE,) * 4,
        scratch_shapes=[
            pltpu.VMEM((rows, tokens), BF16),
            pltpu.VMEM((rows, columns), BF16),
            pltpu.SemaphoreType.DMA,
            pltpu.SemaphoreType.DMA((blocks + 1,)),
        ],
        compiler_params=params(2 * rows * (columns + tokens)),
        cost_estimate=cost,
        name="activate",
    )(*choices, weight, total)
    act_own, state_own = pl.pallas_call(
        functools.partial(second_kernel, width),
        out_shape=outs,
        in_specs=[WHOLE] * 3,
        out_specs=(WHOLE,) * 2,
        compiler_params=params(0),
        cost_estimate=cost,
        name="activate",
    )(turned, rest, total)
    return act_other, state_other, act_own, state_own


def within_kernel(width, *refs):
    tokens, columns = refs[0].shape
    causal = lax.broadcasted_iota(jnp.int32, (tokens, tokens), 0) >= lax.broadcasted_iota(
        jnp.int32, (tokens, tokens), 1
    )
    refs[4][...] = jnp.zeros_like(refs[4])
    for act_ref, within_ref in ((refs[0], refs[2]), (refs[1], refs[3])):
        for h in range(columns // (PARTS * width)):
            at = h * PARTS * width
            queries = act_ref[:, at : at + width]
            keys = act_ref[:, at + width : at + 2 * width]
            values = act_ref[:, at + 2 * width : at + 3 * width]
            scores = lax.dot_general(
                queries, keys, (((1,), (1,)), ((), ())), preferred_element_type=F32
            )
            scores = jnp.where(causal, scores, 0.0).astype(BF16)
            within_ref[:, h * width : (h + 1) * width] = jnp.dot(
                scores, values, preferred_element_type=F32
            )


def attend_within(act_other, act_own, width):
    tokens, columns = act_own.shape
    heads = columns // (PARTS * width)
    return pl.pallas_call(
        functools.partial(within_kernel, width),
        out_shape=(pltpu.VMEM((tokens, heads * width), F32),) * 2 + (pltpu.VMEM((8, 128), F32),),
        in_specs=[WHOLE] * 2,
        out_specs=(WHOLE,) * 3,
        compiler_params=params(0),
        cost_estimate=pl.CostEstimate(
            flops=8 * heads * tokens * tokens * width,
            bytes_accessed=tokens * columns * 4,
            transcendentals=0,
        ),
        name="within",
    )(act_other, act_own)


def across_kernel(
    act_other, act_own, within_other, within_own, prior, other, own, att_ref, square_ref
):
    half, width, _ = own.shape
    core = lax.axis_index("context") % 2
    sides = (
        (1 - core, act_other, within_other, other),
        (core, act_own, within_own, own),
    )
    squares = None
    for h in range(half):
        for side, act, within, earlier in sides:
            head = side * half + h
            carried = prior[head] + earlier[h]
            upper = carried.astype(BF16)
            lower = (carried - upper.astype(F32)).astype(BF16)
            at = h * PARTS * width
            queries = act[:, at : at + width]
            attended = within[:, h * width : (h + 1) * width] + jnp.dot(
                jnp.concatenate([queries, queries], axis=1),
                jnp.concatenate([upper, lower], axis=0),
                preferred_element_type=F32,
            )
            att_ref[:, pl.ds(pl.multiple_of(head * width, width), width)] = attended
            square = attended * attended
            squares = square if squares is None else squares + square
    square_ref[...] = lax.dot_general(
        jnp.ones((8, width), F32),
        squares,
        (((1,), (1,)), ((), ())),
        preferred_element_type=F32,
        precision=lax.Precision.HIGHEST,
    )


def attend_across(acts, withins, prior, other, own):
    tokens = acts[0].shape[0]
    heads, width, _ = prior.shape
    return pl.pallas_call(
        across_kernel,
        out_shape=(
            pltpu.VMEM((tokens, heads * width), F32),
            jax.ShapeDtypeStruct((8, tokens), F32),
        ),
        in_specs=[WHOLE] * 7,
        out_specs=(WHOLE, WHOLE),
        compiler_params=params(0),
        cost_estimate=pl.CostEstimate(
            flops=4 * heads * tokens * width * width, bytes_accessed=0, transcendentals=0
        ),
        name="across",
    )(*acts, *withins, prior, other, own)


def norm_kernel(features, att_ref, gain_ref, *refs):
    out_ref = refs[-1]
    squares = sum(ref[...] for ref in refs[1:-1]) + refs[0][...]
    ones = jnp.ones((squares.shape[0], 128), F32)
    mean_sq = lax.dot_general(
        squares * (1.0 / squares.shape[0] / features),
        ones,
        (((0,), (0,)), ((), ())),
        preferred_element_type=F32,
        precision=lax.Precision.HIGHEST,
    )
    inverse = lax.rsqrt(mean_sq + EPSILON)
    for at in range(0, att_ref.shape[1], 128):
        out_ref[:, at : at + 128] = (
            att_ref[:, at : at + 128] * inverse * gain_ref[:, at : at + 128]
        ).astype(BF16)


def normalize(att, squares, gain, features):
    tokens, columns = att.shape
    return pl.pallas_call(
        functools.partial(norm_kernel, features),
        out_shape=jax.ShapeDtypeStruct((tokens, columns), BF16),
        in_specs=[WHOLE] * (2 + len(squares)),
        out_specs=WHOLE,
        compiler_params=params(0),
        cost_estimate=pl.CostEstimate(
            flops=2 * tokens * columns, bytes_accessed=2 * tokens * columns, transcendentals=0
        ),
        name="normalize",
    )(att, gain[None, :], *squares)


def terms_over_tensor(x, n):
    if n <= 4:
        return [x] + [
            lax.ppermute(x, "tensor", [(i, (i + d) % n) for i in range(n)]) for d in range(1, n)
        ]
    if n & (n - 1):
        return [lax.psum(x, "tensor")]
    bit = 1
    while bit * 2 < n:
        x = x + lax.ppermute(x, "tensor", [(i, i ^ bit) for i in range(n)])
        bit *= 2
    return [x, lax.ppermute(x, "tensor", [(i, i ^ bit) for i in range(n)])]


def meet_kernel(bits, n_up, n_down, final, *refs):
    own, theirs = refs[0], refs[1]
    ups, downs = refs[2 : 2 + n_up], refs[2 + n_up : 2 + n_up + n_down]
    index = lax.axis_index("context")
    core, chip = index % 2, index // 2
    cut = own.shape[0] // 2

    def has(bit):
        return chip // bit % 2 == 1

    for h in range(own.shape[0]):
        total = own[h] + theirs[h]
        before = jnp.zeros_like(total)
        if h < cut:
            for bit, ref in zip(bits, ups):
                got = ref[h].astype(F32)
                before = before + jnp.where(has(bit), got, 0.0)
                total = total + got
            message = total
        else:
            for ref in downs:
                before = before + ref[h - cut].astype(F32)
            message = total
            if n_down and not final:
                message = before + jnp.where(has(bits[-1 - n_down]), 0.0, total)
        if final:
            for_mate, mine = refs[-2:]
            for_mate[h] = before + jnp.where(core == 0, own[h], 0.0)
            mine[h] = before + jnp.where(core == 1, theirs[h], 0.0)
        elif h < cut:
            refs[-2][h] = message.astype(BF16)
        else:
            refs[-1][h - cut] = message.astype(BF16)


def meet(bits, own, theirs, ups, downs, after, final):
    half, width, _ = own.shape
    cut = half // 2
    if final:
        out_shape = [pltpu.VMEM(own.shape, F32)] * 2
    else:
        out_shape = [
            pltpu.VMEM((n, width, width), BF16) for n in (cut, half - cut) if n
        ]
    operands = [own, theirs] + ups + downs + after
    return pl.pallas_call(
        functools.partial(meet_kernel, bits, len(ups), len(downs), final),
        out_shape=out_shape,
        in_specs=[WHOLE] * len(operands),
        out_specs=[WHOLE] * len(out_shape),
        compiler_params=params(0),
        cost_estimate=pl.CostEstimate(
            flops=4 * half * width * width, bytes_accessed=0, transcendentals=0
        ),
        name="meet",
    )(*operands)


def earlier_states(other_states, own, after, n):
    chips, cut = n // 2, own.shape[0] // 2
    swap = [(i, i ^ 1) for i in range(n)]
    theirs = lax.ppermute(other_states, "context", swap)
    bits = [1 << b for b in range((chips - 1).bit_length())]

    def send(x, bit, both):
        pairs = [
            (2 * i + c, 2 * (i ^ bit) + c)
            for i in range(chips)
            for c in range(2)
            if both or not i & bit
        ]
        return lax.ppermute(x, "context", pairs)

    ups, downs = [], []
    for step, (rise, fall) in enumerate(zip(bits, bits[::-1])):
        messages = meet(bits, own, theirs, ups, downs, after if step == 1 else [], False)
        if cut:
            ups = ups + [send(messages[0], rise, step < len(bits) - 1)]
        downs = downs + [send(messages[-1], fall, step > 0)]
    for_mate, mine = meet(bits, own, theirs, ups, downs, [], True)
    return lax.ppermute(for_mate, "context", swap), mine


def hops(n):
    pairs = [[[] for _ in range(n - 1)] for _ in range(2)]
    arrivals = [[] for _ in range(n)]
    for t in range(n - 1):
        for chain in range(2):
            for share in range(n):
                way = 1 if share % 2 == chain else -1
                here = share + way * t
                if 0 <= here < n and 0 <= here + way < n:
                    pairs[chain][t].append((here, here + way))
                    arrivals[here + way].append((t, chain, share))
    return pairs, arrivals


def body(n_tensor, n_context, tokens_t, qkv_weight, prior_state, norm_gain):
    share = tokens_t.shape[0]
    heads, width, _ = prior_state.shape
    early = share // 2

    def cut(x):
        return [x[:early], x[early:]]

    pairs, arrivals = hops(n_tensor)
    starts = [i * share for i in range(n_tensor)]
    total, done = project([[tokens_t]], [0] * n_tensor, starts, qkv_weight, None)
    held = [[tokens_t], [tokens_t]]
    came = {}
    for t in range(n_tensor - 1):
        for chain in range(2):
            if t == 1:
                held[chain], _ = lax.optimization_barrier((held[chain], done))
            if t == 1 and chain == 0:
                held[0] = cut(held[0][0])
            if pairs[chain][t]:
                held[chain] = [lax.ppermute(x, "tensor", pairs[chain][t]) for x in held[chain]]
                came[t, chain] = held[chain]

    for m in range(n_tensor - 1):
        keys = sorted({came_at[m][:2] for came_at in arrivals})
        picks = [keys.index(came_at[m][:2]) for came_at in arrivals]
        rows = [came_at[m][2] * share for came_at in arrivals]
        choices = [came[key] for key in keys]
        if m < n_tensor - 2:
            total, _ = project(choices, picks, rows, qkv_weight, total)
        else:
            choices = [c if len(c) == 2 else cut(c[0]) for c in choices]
            total, _ = project([c[:1] for c in choices], picks, rows, qkv_weight, total)
            rows = [row + early for row in rows]
            other_act, other_states, own_act, own_states = activate(
                [c[1] for c in choices], picks, rows, qkv_weight, total, heads, width
            )
    acts = (other_act, own_act)
    *withins, done = attend_within(*acts, width)
    other, own = earlier_states(other_states, own_states, [done], n_context)
    att, squares = attend_across(acts, withins, prior_state, other, own)
    squares = terms_over_tensor(squares, n_tensor)
    return normalize(att, squares, norm_gain, n_tensor * heads * width)


def solution(mesh):
    n_tensor, n_context = mesh.shape["tensor"], mesh.shape["context"]
    in_specs = (P("tensor", "context"), P(None, "tensor"), P("tensor", None, None), P("tensor"))
    return jax.shard_map(
        functools.partial(body, n_tensor, n_context),
        mesh=mesh,
        in_specs=in_specs,
        out_specs=P("context", "tensor"),
        check_vma=False,
    )
```

```python
import functools

import jax
import jax.numpy as jnp
from jax import lax
from jax.experimental import pallas as pl
from jax.experimental.pallas import tpu as pltpu
from jax.sharding import PartitionSpec as P

EPSILON = 1e-06
PARTS = 3
COLUMNS = 1024
SLOTS = 3
VMEM_EXTRA = 4 * 1024 * 1024

F32 = jnp.float32
BF16 = jnp.bfloat16


def params(scratch):
    return pltpu.CompilerParams(vmem_limit_bytes=scratch + VMEM_EXTRA)


HBM = pl.BlockSpec(memory_space=pltpu.HBM)
WHOLE = pl.BlockSpec(memory_space=pltpu.VMEM)
ANY = pl.BlockSpec(memory_space=pl.ANY)


def start_features(pick, choices, raw, sem):
    for c, pieces in enumerate(choices):

        @pl.when(pick == c)
        def _(pieces=pieces):
            at = 0
            for piece in pieces:
                there = raw.at[pl.ds(at, piece.shape[0])]
                pltpu.make_async_copy(piece, there, sem).start()
                at += piece.shape[0]


def wait_features(raw, sem):
    pltpu.make_async_copy(raw, raw, sem).wait()


def of_place(values):
    place = lax.axis_index("tensor")
    found = jnp.int32(values[0])
    for i, value in enumerate(values[1:], 1):
        if value != values[0]:
            found = jnp.where(place == i, jnp.int32(value), found)
    return found


def column_blocks(columns):
    width = COLUMNS if columns % COLUMNS == 0 else columns
    return [pl.ds(at, width) for at in range(0, columns, width)]


def project_kernel(counts, first, picks, weight_rows, later_rows, *refs):
    refs = list(refs)
    choices = [[refs.pop(0) for _ in range(count)] for count in counts]
    weight = refs.pop(0)
    if not first:
        refs.pop(0)
    total = refs.pop(0)
    slab, done = (refs.pop(0), refs.pop(0)) if later_rows else (None, None)
    raw, turned, sem, *rest = refs
    rows = raw.shape[0]
    blocks = column_blocks(weight.shape[1])

    start_features(of_place(picks), choices, raw, sem)
    copies = []
    slots = 0
    if weight_rows:
        held, weight_sems = rest
        slots = held.shape[0]
        at = pl.ds(pl.multiple_of(of_place(weight_rows), 16), rows)
        for b, block in enumerate(blocks):
            copies.append(
                pltpu.make_async_copy(
                    weight.at[at, block], held.at[b % slots], weight_sems.at[b]
                )
            )
    if later_rows:
        done[...] = jnp.zeros_like(done)
        later = pl.ds(pl.multiple_of(of_place(later_rows), 16), slab.shape[0])
        slab_copy = pltpu.make_async_copy(
            weight.at[later, :], slab, weight_sems.at[len(blocks)]
        )
    for copy in copies[:slots]:
        copy.start()
    wait_features(raw, sem)
    turned[...] = raw[...].T
    for b, block in enumerate(blocks):
        if weight_rows:
            copies[b].wait()
            matrix = held[b % slots]
        else:
            matrix = weight[0:rows, block]
        product = jnp.dot(turned[...], matrix, preferred_element_type=F32)
        if first:
            total[:, block] = product
        else:
            total[:, block] += product
        if b + slots < len(copies):
            copies[b + slots].start()
        if later_rows and b + slots == len(copies) - 1 + (slots == len(copies)):
            slab_copy.start()
    if later_rows:
        slab_copy.wait()


def project(choices, picks, weight, total, weight_rows=None, later_rows=None, later=0):
    counts = [len(pieces) for pieces in choices]
    rows = sum(piece.shape[0] for piece in choices[0])
    tokens, columns = choices[0][0].shape[1], weight.shape[1]
    first = total is None
    flat = [piece for pieces in choices for piece in pieces]
    operands = flat + [weight] + ([] if first else [total])
    out_shape = [pltpu.VMEM((tokens, columns), F32)]
    if later_rows:
        out_shape += [pltpu.VMEM((later, columns), BF16), pltpu.VMEM((8, 128), F32)]
    scratch = [
        pltpu.VMEM((rows, tokens), BF16),
        pltpu.VMEM((tokens, rows), BF16),
        pltpu.SemaphoreType.DMA,
    ]
    scratch_bytes = 4 * rows * tokens
    if weight_rows:
        blocks = column_blocks(columns)
        slots = min(SLOTS, len(blocks))
        scratch += [
            pltpu.VMEM((slots, rows, blocks[0].size), BF16),
            pltpu.SemaphoreType.DMA((len(blocks) + 1,)),
        ]
        scratch_bytes += 2 * slots * rows * blocks[0].size
    return pl.pallas_call(
        functools.partial(project_kernel, counts, first, picks, weight_rows, later_rows),
        out_shape=out_shape,
        in_specs=[HBM if first else ANY] * len(flat)
        + [HBM if weight_rows else WHOLE]
        + ([] if first else [WHOLE]),
        out_specs=[WHOLE] * len(out_shape),
        scratch_shapes=scratch,
        input_output_aliases={} if first else {len(operands) - 1: 0},
        compiler_params=params(scratch_bytes),
        cost_estimate=pl.CostEstimate(
            flops=2 * tokens * rows * columns,
            bytes_accessed=(rows + later) * columns * 2 + rows * tokens * 2,
            transcendentals=0,
        ),
        name="project",
    )(*operands)


def heads_at_once(half):
    return next(g for g in (4, 2, 1) if half % g == 0)


def activate_heads(side, width, turned, slab, total, act_ref, state_ref):
    half = state_ref.shape[0]
    group = PARTS * width
    at_once = heads_at_once(half)
    for h in range(0, half, at_once):
        here = slice(h * group, (h + at_once) * group)
        column = pl.multiple_of((side * half + h) * group, group)
        block = pl.ds(column, at_once * group)
        projected = total[:, block] + jnp.dot(
            turned[...],
            slab[slab.shape[0] - turned.shape[1] :, block],
            preferred_element_type=F32,
        )
        act = (projected / (1.0 + jnp.exp(-projected))).astype(BF16)
        act_ref[:, here] = act
        for g in range(at_once):
            at = g * group
            state_ref[h + g] = lax.dot_general(
                act[:, at + width : at + 2 * width],
                act[:, at + 2 * width : at + group],
                (((0,), (0,)), ((), ())),
                preferred_element_type=F32,
            )


def first_kernel(n_choices, width, picks, *refs):
    choices = refs[:n_choices]
    slab, total, turned, act_ref, state_ref = refs[n_choices:]
    pick = of_place(picks)
    for c, choice in enumerate(choices):

        @pl.when(pick == c)
        def _(choice=choice):
            turned[...] = choice[...].T

    side = 1 - lax.axis_index("context") % 2
    activate_heads(side, width, turned, slab, total, act_ref, state_ref)


def second_kernel(width, turned, slab, total, act_ref, state_ref):
    side = lax.axis_index("context") % 2
    activate_heads(side, width, turned, slab, total, act_ref, state_ref)


def activate(choices, picks, slab, total, heads, width):
    rows, tokens = choices[0].shape
    half = heads // 2
    columns = half * PARTS * width
    outs = (
        pltpu.VMEM((tokens, columns), BF16),
        pltpu.VMEM((half, width, width), F32),
    )
    cost = pl.CostEstimate(
        flops=2 * tokens * rows * columns + 2 * half * tokens * width * width,
        bytes_accessed=rows * tokens * 2,
        transcendentals=tokens * columns,
    )
    turned, act_other, state_other = pl.pallas_call(
        functools.partial(first_kernel, len(choices), width, picks),
        out_shape=(pltpu.VMEM((tokens, rows), BF16),) + outs,
        in_specs=[WHOLE] * (len(choices) + 2),
        out_specs=(WHOLE,) * 3,
        compiler_params=params(0),
        cost_estimate=cost,
        name="activate",
    )(*choices, slab, total)
    act_own, state_own = pl.pallas_call(
        functools.partial(second_kernel, width),
        out_shape=outs,
        in_specs=[WHOLE] * 3,
        out_specs=(WHOLE,) * 2,
        compiler_params=params(0),
        cost_estimate=cost,
        name="activate",
    )(turned, slab, total)
    return act_other, state_other, act_own, state_own


def within_kernel(width, *refs):
    tokens, columns = refs[0].shape
    causal = lax.broadcasted_iota(jnp.int32, (tokens, tokens), 0) >= lax.broadcasted_iota(
        jnp.int32, (tokens, tokens), 1
    )
    refs[4][...] = jnp.zeros_like(refs[4])
    for act_ref, within_ref in ((refs[0], refs[2]), (refs[1], refs[3])):
        for h in range(columns // (PARTS * width)):
            at = h * PARTS * width
            queries = act_ref[:, at : at + width]
            keys = act_ref[:, at + width : at + 2 * width]
            values = act_ref[:, at + 2 * width : at + 3 * width]
            scores = lax.dot_general(
                queries, keys, (((1,), (1,)), ((), ())), preferred_element_type=F32
            )
            scores = jnp.where(causal, scores, 0.0).astype(BF16)
            within_ref[:, h * width : (h + 1) * width] = jnp.dot(
                scores, values, preferred_element_type=F32
            )


def attend_within(act_other, act_own, width):
    tokens, columns = act_own.shape
    heads = columns // (PARTS * width)
    return pl.pallas_call(
        functools.partial(within_kernel, width),
        out_shape=(pltpu.VMEM((tokens, heads * width), F32),) * 2 + (pltpu.VMEM((8, 128), F32),),
        in_specs=[WHOLE] * 2,
        out_specs=(WHOLE,) * 3,
        compiler_params=params(0),
        cost_estimate=pl.CostEstimate(
            flops=8 * heads * tokens * tokens * width,
            bytes_accessed=tokens * columns * 4,
            transcendentals=0,
        ),
        name="within",
    )(act_other, act_own)


def across_kernel(
    act_other, act_own, within_other, within_own, prior, other, own, att_ref, square_ref
):
    half, width, _ = own.shape
    core = lax.axis_index("context") % 2
    sides = (
        (1 - core, act_other, within_other, other),
        (core, act_own, within_own, own),
    )
    squares = None
    for h in range(half):
        for side, act, within, earlier in sides:
            head = side * half + h
            carried = prior[head] + earlier[h]
            upper = carried.astype(BF16)
            lower = (carried - upper.astype(F32)).astype(BF16)
            at = h * PARTS * width
            queries = act[:, at : at + width]
            attended = within[:, h * width : (h + 1) * width] + jnp.dot(
                jnp.concatenate([queries, queries], axis=1),
                jnp.concatenate([upper, lower], axis=0),
                preferred_element_type=F32,
            )
            att_ref[:, pl.ds(pl.multiple_of(head * width, width), width)] = attended
            square = attended * attended
            squares = square if squares is None else squares + square
    square_ref[...] = lax.dot_general(
        jnp.ones((8, width), F32),
        squares,
        (((1,), (1,)), ((), ())),
        preferred_element_type=F32,
        precision=lax.Precision.HIGHEST,
    )


def attend_across(acts, withins, prior, other, own):
    tokens = acts[0].shape[0]
    heads, width, _ = prior.shape
    return pl.pallas_call(
        across_kernel,
        out_shape=(
            pltpu.VMEM((tokens, heads * width), F32),
            jax.ShapeDtypeStruct((8, tokens), F32),
        ),
        in_specs=[WHOLE] * 7,
        out_specs=(WHOLE, WHOLE),
        compiler_params=params(0),
        cost_estimate=pl.CostEstimate(
            flops=4 * heads * tokens * width * width, bytes_accessed=0, transcendentals=0
        ),
        name="across",
    )(*acts, *withins, prior, other, own)


def norm_kernel(features, att_ref, gain_ref, *refs):
    out_ref = refs[-1]
    squares = sum(ref[...] for ref in refs[1:-1]) + refs[0][...]
    ones = jnp.ones((squares.shape[0], 128), F32)
    mean_sq = lax.dot_general(
        squares * (1.0 / squares.shape[0] / features),
        ones,
        (((0,), (0,)), ((), ())),
        preferred_element_type=F32,
        precision=lax.Precision.HIGHEST,
    )
    inverse = lax.rsqrt(mean_sq + EPSILON)
    for at in range(0, att_ref.shape[1], 128):
        out_ref[:, at : at + 128] = (
            att_ref[:, at : at + 128] * inverse * gain_ref[:, at : at + 128]
        ).astype(BF16)


def normalize(att, squares, gain, features):
    tokens, columns = att.shape
    return pl.pallas_call(
        functools.partial(norm_kernel, features),
        out_shape=jax.ShapeDtypeStruct((tokens, columns), BF16),
        in_specs=[WHOLE] * (2 + len(squares)),
        out_specs=WHOLE,
        compiler_params=params(0),
        cost_estimate=pl.CostEstimate(
            flops=2 * tokens * columns, bytes_accessed=2 * tokens * columns, transcendentals=0
        ),
        name="normalize",
    )(att, gain[None, :], *squares)


def terms_over_tensor(x, n):
    if n <= 4:
        return [x] + [
            lax.ppermute(x, "tensor", [(i, (i + d) % n) for i in range(n)]) for d in range(1, n)
        ]
    if n & (n - 1):
        return [lax.psum(x, "tensor")]
    bit = 1
    while bit * 2 < n:
        x = x + lax.ppermute(x, "tensor", [(i, i ^ bit) for i in range(n)])
        bit *= 2
    return [x, lax.ppermute(x, "tensor", [(i, i ^ bit) for i in range(n)])]


def meet_kernel(bits, n_up, n_down, final, *refs):
    own, theirs = refs[0], refs[1]
    ups, downs = refs[2 : 2 + n_up], refs[2 + n_up : 2 + n_up + n_down]
    index = lax.axis_index("context")
    core, chip = index % 2, index // 2
    cut = own.shape[0] // 2

    def has(bit):
        return chip // bit % 2 == 1

    for h in range(own.shape[0]):
        total = own[h] + theirs[h]
        before = jnp.zeros_like(total)
        if h < cut:
            for bit, ref in zip(bits, ups):
                got = ref[h].astype(F32)
                before = before + jnp.where(has(bit), got, 0.0)
                total = total + got
            message = total
        else:
            for ref in downs:
                before = before + ref[h - cut].astype(F32)
            if not final:
                message = before + jnp.where(has(bits[-1 - n_down]), 0.0, total)
        if final:
            for_mate, mine = refs[-2:]
            for_mate[h] = before + jnp.where(core == 0, own[h], 0.0)
            mine[h] = before + jnp.where(core == 1, theirs[h], 0.0)
        elif h < cut:
            refs[-2][h] = message.astype(BF16)
        else:
            refs[-1][h - cut] = message.astype(BF16)


def meet(bits, own, theirs, ups, downs, after, final):
    half, width, _ = own.shape
    cut = half // 2
    if final:
        out_shape = [pltpu.VMEM(own.shape, F32)] * 2
    else:
        out_shape = [
            pltpu.VMEM((n, width, width), BF16) for n in (cut, half - cut) if n
        ]
    operands = [own, theirs] + ups + downs + after
    return pl.pallas_call(
        functools.partial(meet_kernel, bits, len(ups), len(downs), final),
        out_shape=out_shape,
        in_specs=[WHOLE] * len(operands),
        out_specs=[WHOLE] * len(out_shape),
        compiler_params=params(0),
        cost_estimate=pl.CostEstimate(
            flops=4 * half * width * width, bytes_accessed=0, transcendentals=0
        ),
        name="meet",
    )(*operands)


def earlier_states(other_states, own, after, n):
    chips, cut = n // 2, own.shape[0] // 2
    swap = [(i, i ^ 1) for i in range(n)]
    theirs = lax.ppermute(other_states, "context", swap)
    bits = [1 << b for b in range((chips - 1).bit_length())]

    def send(x, bit):
        pairs = [(2 * i + c, 2 * (i ^ bit) + c) for i in range(chips) for c in range(2)]
        return lax.ppermute(x, "context", pairs)

    ups, downs = [], []
    for step, (rise, fall) in enumerate(zip(bits, bits[::-1])):
        messages = meet(bits, own, theirs, ups, downs, after if step == 1 else [], False)
        if cut:
            ups = ups + [send(messages[0], rise)]
        downs = downs + [send(messages[-1], fall)]
    for_mate, mine = meet(bits, own, theirs, ups, downs, [], True)
    return lax.ppermute(for_mate, "context", swap), mine


def hops(n):
    pairs = [[[] for _ in range(n - 1)] for _ in range(2)]
    arrivals = [[] for _ in range(n)]
    for t in range(n - 1):
        for chain in range(2):
            for share in range(n):
                way = 1 if share % 2 == chain else -1
                here = share + way * t
                if 0 <= here < n and 0 <= here + way < n:
                    pairs[chain][t].append((here, here + way))
                    if t == 1 and chain == 1:
                        pairs[chain][t].append((here + way, here))
                    arrivals[here + way].append((t, chain, share))
    pairs = [[sorted(set(p)) for p in chain] for chain in pairs]
    return pairs, arrivals


def body(n_tensor, n_context, tokens_t, qkv_weight, prior_state, norm_gain):
    share = tokens_t.shape[0]
    heads, width, _ = prior_state.shape
    early = share // 2

    def cut(x):
        return [x[:early], x[early:]]

    pairs, arrivals = hops(n_tensor)
    last = n_tensor - 2
    total, slab, done = project(
        [[tokens_t]],
        [0] * n_tensor,
        qkv_weight,
        None,
        [i * share for i in range(n_tensor)],
        [there[last][2] * share for there in arrivals],
        share,
    )
    held = [[tokens_t], [tokens_t]]
    came = {}
    for t in range(n_tensor - 1):
        for chain in range(2):
            if t == 1:
                held[chain], _ = lax.optimization_barrier((held[chain], done))
            if t == 1 and chain == 0:
                held[0] = cut(held[0][0])
            if pairs[chain][t]:
                held[chain] = [lax.ppermute(x, "tensor", pairs[chain][t]) for x in held[chain]]
                came[t, chain] = held[chain]

    for m in range(n_tensor - 1):
        keys = sorted({there[m][:2] for there in arrivals})
        picks = [keys.index(there[m][:2]) for there in arrivals]
        choices = [came[key] for key in keys]
        if m < last:
            rows = [there[m][2] * share for there in arrivals]
            (total,) = project(choices, picks, qkv_weight, total, rows)
        else:
            choices = [c if len(c) == 2 else cut(c[0]) for c in choices]
            (total,) = project([c[:1] for c in choices], picks, slab, total)
    other_act, other_states, own_act, own_states = activate(
        [c[1] for c in choices], picks, slab, total, heads, width
    )
    acts = (other_act, own_act)
    *withins, done = attend_within(*acts, width)
    other, own = earlier_states(other_states, own_states, [done], n_context)
    att, squares = attend_across(acts, withins, prior_state, other, own)
    squares = terms_over_tensor(squares, n_tensor)
    return normalize(att, squares, norm_gain, n_tensor * heads * width)


def solution(mesh):
    n_tensor, n_context = mesh.shape["tensor"], mesh.shape["context"]
    in_specs = (P("tensor", "context"), P(None, "tensor"), P("tensor", None, None), P("tensor"))
    return jax.shard_map(
        functools.partial(body, n_tensor, n_context),
        mesh=mesh,
        in_specs=in_specs,
        out_specs=P("context", "tensor"),
        check_vma=False,
    )
```

```python
import functools

import jax
import jax.numpy as jnp
from jax import lax
from jax.experimental import pallas as pl
from jax.experimental.pallas import tpu as pltpu
from jax.sharding import PartitionSpec as P

EPSILON = 1e-06
PARTS = 3
COLUMNS = 1024
SLOT_BYTES = 10 * 1024 * 1024
VMEM_EXTRA = 4 * 1024 * 1024

F32 = jnp.float32
BF16 = jnp.bfloat16


def params(scratch):
    return pltpu.CompilerParams(vmem_limit_bytes=scratch + VMEM_EXTRA)


HBM = pl.BlockSpec(memory_space=pltpu.HBM)
WHOLE = pl.BlockSpec(memory_space=pltpu.VMEM)
ANY = pl.BlockSpec(memory_space=pl.ANY)


def start_features(pick, choices, raw, sem):
    for c, pieces in enumerate(choices):

        @pl.when(pick == c)
        def _(pieces=pieces):
            at = 0
            for piece in pieces:
                there = raw.at[pl.ds(at, piece.shape[0])]
                pltpu.make_async_copy(piece, there, sem).start()
                at += piece.shape[0]


def wait_features(raw, sem):
    pltpu.make_async_copy(raw, raw, sem).wait()


def of_place(values):
    place = lax.axis_index("tensor")
    found = jnp.int32(values[0])
    for i, value in enumerate(values[1:], 1):
        if value != values[0]:
            found = jnp.where(place == i, jnp.int32(value), found)
    return found


def column_blocks(columns):
    width = COLUMNS if columns % COLUMNS == 0 else columns
    return [pl.ds(at, width) for at in range(0, columns, width)]


def project_kernel(counts, first, picks, weight_rows, next_rows, slab_rows, *refs):
    refs = list(refs)
    choices = [[refs.pop(0) for _ in range(count)] for count in counts]
    weight = refs.pop(0)
    ready = None
    if not first:
        ready, _, _ = refs.pop(0), refs.pop(0), refs.pop(0)
    total, done = refs.pop(0), refs.pop(0)
    next_block = refs.pop(0) if next_rows else None
    slab = refs.pop(0) if slab_rows else None
    raw, turned, held, sem, weight_sems = refs
    done[...] = jnp.zeros_like(done)
    rows = raw.shape[0]
    slots = held.shape[0]
    blocks = column_blocks(weight.shape[1])

    start_features(of_place(picks), choices, raw, sem)
    at = pl.ds(pl.multiple_of(of_place(weight_rows), 16), rows)
    streamed = blocks if first else blocks[1:]
    copies = [
        pltpu.make_async_copy(weight.at[at, block], held.at[b % slots], weight_sems.at[b])
        for b, block in enumerate(streamed)
    ]
    if next_rows:
        at = pl.ds(pl.multiple_of(of_place(next_rows), 16), next_block.shape[0])
        copies.append(
            pltpu.make_async_copy(
                weight.at[at, blocks[0]], next_block, weight_sems.at[len(streamed)]
            )
        )
    if slab_rows:
        at = pl.ds(pl.multiple_of(of_place(slab_rows), 16), slab.shape[0])
        copies.append(
            pltpu.make_async_copy(weight.at[at, :], slab, weight_sems.at[len(copies)])
        )
    for copy in copies[:slots]:
        copy.start()
    wait_features(raw, sem)
    turned[...] = raw[...].T
    for b, block in enumerate(blocks):
        b = b if first else b - 1
        if b < 0:
            matrix = ready[...]
        else:
            copies[b].wait()
            matrix = held[b % slots]
        product = jnp.dot(turned[...], matrix, preferred_element_type=F32)
        if first:
            total[:, block] = product
        else:
            total[:, block] += product
        if 0 <= b < len(copies) - slots:
            copies[b + slots].start()
    for copy in copies[len(streamed) :]:
        copy.wait()


def project(
    choices,
    picks,
    weight,
    weight_rows,
    ready,
    total,
    after,
    next_rows=None,
    next_count=0,
    slab_rows=None,
    slab_count=0,
):
    counts = [len(pieces) for pieces in choices]
    rows = sum(piece.shape[0] for piece in choices[0])
    tokens, columns = choices[0][0].shape[1], weight.shape[1]
    first = total is None
    flat = [piece for pieces in choices for piece in pieces]
    operands = flat + [weight] + ([] if first else [ready, after, total])
    blocks = column_blocks(columns)
    block = blocks[0].size
    slots = max(1, min(SLOT_BYTES // (2 * rows * block), len(blocks)))
    out_shape = [pltpu.VMEM((tokens, columns), F32), pltpu.VMEM((8, 128), F32)]
    if next_rows:
        out_shape.append(pltpu.VMEM((next_count, block), BF16))
    if slab_rows:
        out_shape.append(pltpu.VMEM((slab_count, columns), BF16))
    return pl.pallas_call(
        functools.partial(
            project_kernel, counts, first, picks, weight_rows, next_rows, slab_rows
        ),
        out_shape=out_shape,
        in_specs=[ANY] * len(flat) + [HBM] + ([] if first else [WHOLE, ANY, WHOLE]),
        out_specs=[WHOLE] * len(out_shape),
        scratch_shapes=[
            pltpu.VMEM((rows, tokens), BF16),
            pltpu.VMEM((tokens, rows), BF16),
            pltpu.VMEM((slots, rows, block), BF16),
            pltpu.SemaphoreType.DMA,
            pltpu.SemaphoreType.DMA((len(blocks) + 2,)),
        ],
        input_output_aliases={} if first else {len(operands) - 1: 0},
        compiler_params=params(2 * rows * (2 * tokens + slots * block)),
        cost_estimate=pl.CostEstimate(
            flops=2 * tokens * rows * columns,
            bytes_accessed=rows * columns * 2 + rows * tokens * 2,
            transcendentals=0,
        ),
        name="project",
    )(*operands)


def gate_kernel(*refs):
    pass


def gate(x, after):
    return pl.pallas_call(
        gate_kernel,
        out_shape=jax.ShapeDtypeStruct(x.shape, x.dtype),
        in_specs=[ANY, ANY],
        out_specs=ANY,
        input_output_aliases={0: 0},
        compiler_params=params(0),
        name="gate",
    )(x, after)


def cut_kernel(x, *refs):
    *_, upper, lower, sems = refs
    rows = upper.shape[0]
    copies = [
        pltpu.make_async_copy(x.at[pl.ds(0, rows)], upper, sems.at[0]),
        pltpu.make_async_copy(x.at[pl.ds(rows, lower.shape[0])], lower, sems.at[1]),
    ]
    for copy in copies:
        copy.start()
    for copy in copies:
        copy.wait()


def cut_in_two(x, rows, after=()):
    sizes = (rows, x.shape[0] - rows)
    return list(
        pl.pallas_call(
            cut_kernel,
            out_shape=[pltpu.VMEM((size, x.shape[1]), x.dtype) for size in sizes],
            in_specs=[ANY if after else HBM] + [ANY] * len(after),
            out_specs=[WHOLE] * 2,
            scratch_shapes=[pltpu.SemaphoreType.DMA((2,))],
            compiler_params=params(0),
            name="cut",
        )(x, *after)
    )


def heads_at_once(half):
    return next(g for g in (4, 2, 1) if half % g == 0)


def activate_heads(side, width, turned, slab, total, act_ref, state_ref):
    half = state_ref.shape[0]
    group = PARTS * width
    at_once = heads_at_once(half)
    for h in range(0, half, at_once):
        here = slice(h * group, (h + at_once) * group)
        column = pl.multiple_of((side * half + h) * group, group)
        block = pl.ds(column, at_once * group)
        projected = total[:, block] + jnp.dot(
            turned[...],
            slab[slab.shape[0] - turned.shape[1] :, block],
            preferred_element_type=F32,
        )
        act = (projected / (1.0 + jnp.exp(-projected))).astype(BF16)
        act_ref[:, here] = act
        for g in range(at_once):
            at = g * group
            state_ref[h + g] = lax.dot_general(
                act[:, at + width : at + 2 * width],
                act[:, at + 2 * width : at + group],
                (((0,), (0,)), ((), ())),
                preferred_element_type=F32,
            )


def first_kernel(n_choices, width, picks, *refs):
    choices = refs[:n_choices]
    slab, total, turned, act_ref, state_ref = refs[n_choices:]
    pick = of_place(picks)
    for c, choice in enumerate(choices):

        @pl.when(pick == c)
        def _(choice=choice):
            turned[...] = choice[...].T

    side = 1 - lax.axis_index("context") % 2
    activate_heads(side, width, turned, slab, total, act_ref, state_ref)


def second_kernel(width, turned, slab, total, act_ref, state_ref):
    side = lax.axis_index("context") % 2
    activate_heads(side, width, turned, slab, total, act_ref, state_ref)


def activate(choices, picks, slab, total, heads, width):
    rows, tokens = choices[0].shape
    half = heads // 2
    columns = half * PARTS * width
    outs = (
        pltpu.VMEM((tokens, columns), BF16),
        pltpu.VMEM((half, width, width), F32),
    )
    cost = pl.CostEstimate(
        flops=2 * tokens * rows * columns + 2 * half * tokens * width * width,
        bytes_accessed=rows * tokens * 2,
        transcendentals=tokens * columns,
    )
    turned, act_other, state_other = pl.pallas_call(
        functools.partial(first_kernel, len(choices), width, picks),
        out_shape=(pltpu.VMEM((tokens, rows), BF16),) + outs,
        in_specs=[WHOLE] * (len(choices) + 2),
        out_specs=(WHOLE,) * 3,
        compiler_params=params(0),
        cost_estimate=cost,
        name="activate",
    )(*choices, slab, total)
    act_own, state_own = pl.pallas_call(
        functools.partial(second_kernel, width),
        out_shape=outs,
        in_specs=[WHOLE] * 3,
        out_specs=(WHOLE,) * 2,
        compiler_params=params(0),
        cost_estimate=cost,
        name="activate",
    )(turned, slab, total)
    return act_other, state_other, act_own, state_own


def within_kernel(width, *refs):
    tokens, columns = refs[0].shape
    causal = lax.broadcasted_iota(jnp.int32, (tokens, tokens), 0) >= lax.broadcasted_iota(
        jnp.int32, (tokens, tokens), 1
    )
    refs[4][...] = jnp.zeros_like(refs[4])
    for act_ref, within_ref in ((refs[0], refs[2]), (refs[1], refs[3])):
        for h in range(columns // (PARTS * width)):
            at = h * PARTS * width
            queries = act_ref[:, at : at + width]
            keys = act_ref[:, at + width : at + 2 * width]
            values = act_ref[:, at + 2 * width : at + 3 * width]
            scores = lax.dot_general(
                queries, keys, (((1,), (1,)), ((), ())), preferred_element_type=F32
            )
            scores = jnp.where(causal, scores, 0.0).astype(BF16)
            within_ref[:, h * width : (h + 1) * width] = jnp.dot(
                scores, values, preferred_element_type=F32
            )


def attend_within(act_other, act_own, width):
    tokens, columns = act_own.shape
    heads = columns // (PARTS * width)
    return pl.pallas_call(
        functools.partial(within_kernel, width),
        out_shape=(pltpu.VMEM((tokens, heads * width), F32),) * 2 + (pltpu.VMEM((8, 128), F32),),
        in_specs=[WHOLE] * 2,
        out_specs=(WHOLE,) * 3,
        compiler_params=params(0),
        cost_estimate=pl.CostEstimate(
            flops=8 * heads * tokens * tokens * width,
            bytes_accessed=tokens * columns * 4,
            transcendentals=0,
        ),
        name="within",
    )(act_other, act_own)


def across_kernel(own_side, n_groups, act, within, prior, *refs):
    groups = refs[:n_groups]
    *squares_in, att_ref, square_ref = refs[n_groups:]
    places = [(ref, h) for ref in groups for h in range(ref.shape[0])]
    half, width = len(places), prior.shape[1]
    core = lax.axis_index("context") % 2
    side = core if own_side else 1 - core
    squares = None
    for h, (earlier, place) in enumerate(places):
        carried = prior[side * half + h] + earlier[place]
        upper = carried.astype(BF16)
        lower = (carried - upper.astype(F32)).astype(BF16)
        at = h * PARTS * width
        queries = act[:, at : at + width]
        here = slice(h * width, (h + 1) * width)
        attended = within[:, here] + jnp.dot(
            jnp.concatenate([queries, queries], axis=1),
            jnp.concatenate([upper, lower], axis=0),
            preferred_element_type=F32,
        )
        att_ref[:, here] = attended
        square = attended * attended
        squares = square if squares is None else squares + square
    total = lax.dot_general(
        jnp.ones((8, width), F32),
        squares,
        (((1,), (1,)), ((), ())),
        preferred_element_type=F32,
        precision=lax.Precision.HIGHEST,
    )
    for ref in squares_in:
        total += ref[...]
    square_ref[...] = total


def attend_across(own_side, act, within, prior, earlier, squares):
    tokens = act.shape[0]
    half, width = prior.shape[0] // 2, prior.shape[1]
    operands = [act, within, prior] + earlier + squares
    return pl.pallas_call(
        functools.partial(across_kernel, own_side, len(earlier)),
        out_shape=(
            pltpu.VMEM((tokens, half * width), F32),
            pltpu.VMEM((8, tokens), F32),
        ),
        in_specs=[WHOLE] * len(operands),
        out_specs=(WHOLE, WHOLE),
        compiler_params=params(0),
        cost_estimate=pl.CostEstimate(
            flops=4 * half * tokens * width * width, bytes_accessed=0, transcendentals=0
        ),
        name="across",
    )(*operands)


def norm_kernel(features, att_other, att_own, gain_ref, *refs):
    *square_refs, out_ref, held, sems = refs
    core = lax.axis_index("context") % 2
    squares = sum(ref[...] for ref in square_refs[1:]) + square_refs[0][...]
    ones = jnp.ones((squares.shape[0], 128), F32)
    mean_sq = lax.dot_general(
        squares * (1.0 / squares.shape[0] / features),
        ones,
        (((0,), (0,)), ((), ())),
        preferred_element_type=F32,
        precision=lax.Precision.HIGHEST,
    )
    inverse = lax.rsqrt(mean_sq + EPSILON)
    columns = held.shape[2]
    parts = att_own.shape[1] // columns
    copies = []
    for side, att in ((1 - core, att_other), (core, att_own)):
        for part in range(parts):
            slot = len(copies)
            first = pl.multiple_of((side * parts + part) * columns, columns)
            for at in range(0, columns, 128):
                gain = gain_ref[:, pl.ds(pl.multiple_of(first + at, 128), 128)]
                here = slice(part * columns + at, part * columns + at + 128)
                held[slot, :, at : at + 128] = (att[:, here] * inverse * gain).astype(BF16)
            copies.append(
                pltpu.make_async_copy(
                    held.at[slot], out_ref.at[:, pl.ds(first, columns)], sems.at[slot]
                )
            )
            copies[-1].start()
    for copy in copies:
        copy.wait()


def normalize(att_other, att_own, squares, gain, features):
    tokens, half = att_own.shape
    columns = half // 2 if half % 256 == 0 else half
    count = 2 * half // columns
    return pl.pallas_call(
        functools.partial(norm_kernel, features),
        out_shape=jax.ShapeDtypeStruct((tokens, 2 * half), BF16),
        in_specs=[WHOLE] * (3 + len(squares)),
        out_specs=HBM,
        scratch_shapes=[
            pltpu.VMEM((count, tokens, columns), BF16),
            pltpu.SemaphoreType.DMA((count,)),
        ],
        compiler_params=params(4 * tokens * half),
        cost_estimate=pl.CostEstimate(
            flops=4 * tokens * half, bytes_accessed=4 * tokens * half, transcendentals=0
        ),
        name="normalize",
    )(att_other, att_own, gain[None, :], *squares)


def terms_over_tensor(x, n):
    if n <= 4:
        return [x] + [
            lax.ppermute(x, "tensor", [(i, (i + d) % n) for i in range(n)]) for d in range(1, n)
        ]
    if n & (n - 1):
        return [lax.psum(x, "tensor")]
    bit = 1
    while bit * 2 < n:
        x = x + lax.ppermute(x, "tensor", [(i, i ^ bit) for i in range(n)])
        bit *= 2
    return [x, lax.ppermute(x, "tensor", [(i, i ^ bit) for i in range(n)])]


def meet_kernel(bits, n_got, first, final, *refs):
    own, theirs, gots = refs[0], refs[1], refs[2 : 2 + n_got]
    index = lax.axis_index("context")
    core, chip = index % 2, index // 2
    rising = core == 0

    def has(bit):
        return chip // bit % 2 == 1

    for h in range(refs[-1].shape[0]):
        own_part, their_part = own[first + h], theirs[first + h]
        total = own_part + their_part
        reached = total
        before = jnp.zeros_like(total)
        for bit, ref in zip(bits, gots):
            got = ref[h].astype(F32)
            earlier = jnp.logical_or(core == 1, has(bit))
            before = before + jnp.where(earlier, got, 0.0)
            reached = reached + got
        if final:
            for_mate, mine = refs[-2:]
            for_mate[h] = before + jnp.where(rising, own_part, 0.0)
            mine[h] = before + jnp.where(rising, 0.0, their_part)
        else:
            falling = before + jnp.where(has(bits[-1 - n_got]), 0.0, total)
            refs[-1][h] = jnp.where(rising, reached, falling).astype(BF16)


def meet(bits, own, theirs, gots, after, first, count, final):
    _, width, _ = own.shape
    if final:
        out_shape = [pltpu.VMEM((count, width, width), F32)] * 2
    else:
        out_shape = [pltpu.VMEM((count, width, width), BF16)]
    operands = [own, theirs] + gots + after
    return pl.pallas_call(
        functools.partial(meet_kernel, bits, len(gots), first, final),
        out_shape=out_shape,
        in_specs=[WHOLE] * len(operands),
        out_specs=[WHOLE] * len(out_shape),
        compiler_params=params(0),
        cost_estimate=pl.CostEstimate(
            flops=4 * count * width * width, bytes_accessed=0, transcendentals=0
        ),
        name="meet",
    )(*operands)


def earlier_states(other_states, own, after, n):
    chips, half = n // 2, own.shape[0]
    swap = [(i, i ^ 1) for i in range(n)]
    theirs = lax.ppermute(other_states, "context", swap)
    bits = [1 << b for b in range((chips - 1).bit_length())]
    groups = [(0, half // 2), (half // 2, half - half // 2)]
    groups = [group for group in groups if group[1]]
    gots = [[] for _ in groups]
    for step, (rise, fall) in enumerate(zip(bits, bits[::-1])):
        pairs = [
            (2 * i + c, 2 * (i ^ bit) + c)
            for i in range(chips)
            for c, bit in enumerate((rise, fall))
        ]
        for g, group in enumerate(groups):
            waits = after if step == 1 and g == 0 else []
            (message,) = meet(bits, own, theirs, gots[g], waits, *group, False)
            gots[g] = gots[g] + [lax.ppermute(message, "context", pairs)]
    others, mine = [], []
    for g, group in enumerate(groups):
        for_mate, kept = meet(bits, own, theirs, gots[g], [], *group, True)
        others.append(lax.ppermute(for_mate, "context", swap))
        mine.append(kept)
    return others, mine


def hops(n):
    pairs = [[[] for _ in range(n - 1)] for _ in range(2)]
    arrivals = [[] for _ in range(n)]
    for t in range(n - 1):
        for chain in range(2):
            for share in range(n):
                way = 1 if share % 2 == chain else -1
                here = share + way * t
                if 0 <= here < n and 0 <= here + way < n:
                    pairs[chain][t].append((here, here + way))
                    if t == 1 and chain == 1:
                        pairs[chain][t].append((here + way, here))
                    arrivals[here + way].append((t, chain, share))
    pairs = [[sorted(set(p)) for p in chain] for chain in pairs]
    return pairs, arrivals


def body(n_tensor, n_context, tokens_t, qkv_weight, prior_state, norm_gain):
    share = tokens_t.shape[0]
    heads, width, _ = prior_state.shape
    early = share // 2

    pairs, arrivals = hops(n_tensor)
    last = n_tensor - 2
    pieces = cut_in_two(tokens_t, early)
    held = [[tokens_t], pieces]
    came = {}

    steps = [(-1, None), (0, None)] + [(1, 0), (1, 1)] + [(m, None) for m in range(2, last)]
    steps = [step for step in steps if step[0] < last] + [(last, 0)]

    def rows_of(m, piece):
        starts = [there[m][2] if m >= 0 else i for i, there in enumerate(arrivals)]
        return [start * share + (early if piece == 1 else 0) for start in starts]

    def count_of(piece):
        return {None: share, 0: early, 1: share - early}[piece]

    def run(number, ready, total, after):
        m, piece = steps[number]
        following = []
        if number + 1 < len(steps):
            following = [rows_of(*steps[number + 1]), count_of(steps[number + 1][1])]
            if number == 0:
                following += [rows_of(last, 1), share - early]
        choices, picks = [pieces], [0] * n_tensor
        if m >= 0:
            keys = sorted({there[m][:2] for there in arrivals})
            picks = [keys.index(there[m][:2]) for there in arrivals]
            choices = [came[key] if piece is None else [came[key][piece]] for key in keys]
        return project(
            choices, picks, qkv_weight, rows_of(m, piece), ready, total, after, *following
        )

    total, done, ready, slab = run(0, None, None, None)
    number = 1
    for t in range(n_tensor - 1):
        for chain in range(2):
            if pairs[chain][t]:
                held[chain] = [lax.ppermute(x, "tensor", pairs[chain][t]) for x in held[chain]]
                came[t, chain] = held[chain]
        if t == 0:
            if (0, 1) in came:
                held[1][0] = done = gate(held[1][0], done)
            held[0] = came[0, 0] = cut_in_two(held[0][0], early, [done])
            if (0, 1) in came:
                held[1][1] = gate(held[1][1], held[0][0])
        gates = [0, 1] if t == 1 and t < last else []
        while number < len(steps) - 1 and 1 <= t >= steps[number][0]:
            total, done, ready = run(number, ready, total, done)
            number += 1
            if gates:
                j = gates.pop(0)
                held[0][j] = done = gate(held[0][j], done)

    total, _ = run(number, ready, total, done)
    keys = sorted({there[last][:2] for there in arrivals})
    picks = [keys.index(there[last][:2]) for there in arrivals]
    choices = [came[key] for key in keys]
    other_act, other_states, own_act, own_states = activate(
        [c[1] for c in choices], picks, slab, total, heads, width
    )
    other_within, own_within, done = attend_within(other_act, own_act, width)
    other, own = earlier_states(other_states, own_states, [done], n_context)
    own_att, squares = attend_across(True, own_act, own_within, prior_state, own, [])
    other_att, squares = attend_across(
        False, other_act, other_within, prior_state, other, [squares]
    )
    squares = terms_over_tensor(squares, n_tensor)
    return normalize(other_att, own_att, squares, norm_gain, n_tensor * heads * width)


def solution(mesh):
    n_tensor, n_context = mesh.shape["tensor"], mesh.shape["context"]
    in_specs = (P("tensor", "context"), P(None, "tensor"), P("tensor", None, None), P("tensor"))
    return jax.shard_map(
        functools.partial(body, n_tensor, n_context),
        mesh=mesh,
        in_specs=in_specs,
        out_specs=P("context", "tensor"),
        check_vma=False,
    )
```

```python
import functools

import jax
import jax.numpy as jnp
from jax import lax
from jax.experimental import pallas as pl
from jax.experimental.pallas import tpu as pltpu
from jax.sharding import PartitionSpec as P

EPSILON = 1e-06
PARTS = 3
COLUMNS = 1024
SLOT_BYTES = 10 * 1024 * 1024
VMEM_EXTRA = 4 * 1024 * 1024

F32 = jnp.float32
BF16 = jnp.bfloat16


def params(scratch):
    return pltpu.CompilerParams(vmem_limit_bytes=scratch + VMEM_EXTRA)


HBM = pl.BlockSpec(memory_space=pltpu.HBM)
WHOLE = pl.BlockSpec(memory_space=pltpu.VMEM)
ANY = pl.BlockSpec(memory_space=pl.ANY)


def start_features(pick, choices, raw, sem):
    for c, pieces in enumerate(choices):

        @pl.when(pick == c)
        def _(pieces=pieces):
            at = 0
            for piece in pieces:
                there = raw.at[pl.ds(at, piece.shape[0])]
                pltpu.make_async_copy(piece, there, sem).start()
                at += piece.shape[0]


def wait_features(raw, sem):
    pltpu.make_async_copy(raw, raw, sem).wait()


def of_place(values):
    place = lax.axis_index("tensor")
    found = jnp.int32(values[0])
    for i, value in enumerate(values[1:], 1):
        if value != values[0]:
            found = jnp.where(place == i, jnp.int32(value), found)
    return found


def column_blocks(columns):
    width = COLUMNS if columns % COLUMNS == 0 else columns
    return [pl.ds(at, width) for at in range(0, columns, width)]


def project_kernel(counts, first, picks, weight_rows, next_rows, slab_rows, *refs):
    refs = list(refs)
    choices = [[refs.pop(0) for _ in range(count)] for count in counts]
    weight = refs.pop(0)
    ready = None
    if not first:
        ready, _, _ = refs.pop(0), refs.pop(0), refs.pop(0)
    total, done = refs.pop(0), refs.pop(0)
    next_block = refs.pop(0) if next_rows else None
    slab = refs.pop(0) if slab_rows else None
    raw, turned, held, sem, weight_sems = refs
    done[...] = jnp.zeros_like(done)
    rows = raw.shape[0]
    slots = held.shape[0]
    blocks = column_blocks(weight.shape[1])

    start_features(of_place(picks), choices, raw, sem)
    at = pl.ds(pl.multiple_of(of_place(weight_rows), 16), rows)
    streamed = blocks if first else blocks[1:]
    copies = [
        pltpu.make_async_copy(weight.at[at, block], held.at[b % slots], weight_sems.at[b])
        for b, block in enumerate(streamed)
    ]
    if next_rows:
        at = pl.ds(pl.multiple_of(of_place(next_rows), 16), next_block.shape[0])
        copies.append(
            pltpu.make_async_copy(
                weight.at[at, blocks[0]], next_block, weight_sems.at[len(streamed)]
            )
        )
    if slab_rows:
        at = pl.ds(pl.multiple_of(of_place(slab_rows), 16), slab.shape[0])
        copies.append(
            pltpu.make_async_copy(weight.at[at, :], slab, weight_sems.at[len(copies)])
        )
    for copy in copies[:slots]:
        copy.start()
    wait_features(raw, sem)
    turned[...] = raw[...].T
    for b, block in enumerate(blocks):
        b = b if first else b - 1
        if b < 0:
            matrix = ready[...]
        else:
            copies[b].wait()
            matrix = held[b % slots]
        product = jnp.dot(turned[...], matrix, preferred_element_type=F32)
        if first:
            total[:, block] = product
        else:
            total[:, block] += product
        if 0 <= b < len(copies) - slots:
            copies[b + slots].start()
    for copy in copies[len(streamed) :]:
        copy.wait()


def project(
    choices,
    picks,
    weight,
    weight_rows,
    ready,
    total,
    after,
    next_rows=None,
    next_count=0,
    slab_rows=None,
    slab_count=0,
):
    counts = [len(pieces) for pieces in choices]
    rows = sum(piece.shape[0] for piece in choices[0])
    tokens, columns = choices[0][0].shape[1], weight.shape[1]
    first = total is None
    flat = [piece for pieces in choices for piece in pieces]
    operands = flat + [weight] + ([] if first else [ready, after, total])
    blocks = column_blocks(columns)
    block = blocks[0].size
    slots = max(1, min(SLOT_BYTES // (2 * rows * block), len(blocks)))
    out_shape = [pltpu.VMEM((tokens, columns), F32), pltpu.VMEM((8, 128), F32)]
    if next_rows:
        out_shape.append(pltpu.VMEM((next_count, block), BF16))
    if slab_rows:
        out_shape.append(pltpu.VMEM((slab_count, columns), BF16))
    return pl.pallas_call(
        functools.partial(
            project_kernel, counts, first, picks, weight_rows, next_rows, slab_rows
        ),
        out_shape=out_shape,
        in_specs=[ANY] * len(flat) + [HBM] + ([] if first else [WHOLE, ANY, WHOLE]),
        out_specs=[WHOLE] * len(out_shape),
        scratch_shapes=[
            pltpu.VMEM((rows, tokens), BF16),
            pltpu.VMEM((tokens, rows), BF16),
            pltpu.VMEM((slots, rows, block), BF16),
            pltpu.SemaphoreType.DMA,
            pltpu.SemaphoreType.DMA((len(blocks) + 2,)),
        ],
        input_output_aliases={} if first else {len(operands) - 1: 0},
        compiler_params=params(2 * rows * (2 * tokens + slots * block)),
        cost_estimate=pl.CostEstimate(
            flops=2 * tokens * rows * columns,
            bytes_accessed=rows * columns * 2 + rows * tokens * 2,
            transcendentals=0,
        ),
        name="project",
    )(*operands)


def gate_kernel(*refs):
    pass


def gate(x, after):
    return pl.pallas_call(
        gate_kernel,
        out_shape=jax.ShapeDtypeStruct(x.shape, x.dtype),
        in_specs=[ANY, ANY],
        out_specs=ANY,
        input_output_aliases={0: 0},
        compiler_params=params(0),
        name="gate",
    )(x, after)


def cut_kernel(x, *refs):
    *_, upper, lower, sems = refs
    rows = upper.shape[0]
    copies = [
        pltpu.make_async_copy(x.at[pl.ds(0, rows)], upper, sems.at[0]),
        pltpu.make_async_copy(x.at[pl.ds(rows, lower.shape[0])], lower, sems.at[1]),
    ]
    for copy in copies:
        copy.start()
    for copy in copies:
        copy.wait()


def cut_in_two(x, rows, after=()):
    sizes = (rows, x.shape[0] - rows)
    return list(
        pl.pallas_call(
            cut_kernel,
            out_shape=[pltpu.VMEM((size, x.shape[1]), x.dtype) for size in sizes],
            in_specs=[ANY if after else HBM] + [ANY] * len(after),
            out_specs=[WHOLE] * 2,
            scratch_shapes=[pltpu.SemaphoreType.DMA((2,))],
            compiler_params=params(0),
            name="cut",
        )(x, *after)
    )


def heads_at_once(half):
    return next(g for g in (4, 2, 1) if half % g == 0)


def activate_heads(side, width, turned, slab, total, act_ref, state_ref):
    half = state_ref.shape[0]
    group = PARTS * width
    at_once = heads_at_once(half)
    for h in range(0, half, at_once):
        here = slice(h * group, (h + at_once) * group)
        column = pl.multiple_of((side * half + h) * group, group)
        block = pl.ds(column, at_once * group)
        projected = total[:, block] + jnp.dot(
            turned[...],
            slab[slab.shape[0] - turned.shape[1] :, block],
            preferred_element_type=F32,
        )
        act = (projected / (1.0 + jnp.exp(-projected))).astype(BF16)
        act_ref[:, here] = act
        for g in range(at_once):
            at = g * group
            state_ref[h + g] = lax.dot_general(
                act[:, at + width : at + 2 * width],
                act[:, at + 2 * width : at + group],
                (((0,), (0,)), ((), ())),
                preferred_element_type=F32,
            )


def first_kernel(n_choices, width, picks, *refs):
    choices = refs[:n_choices]
    slab, total, turned, act_ref, state_ref = refs[n_choices:]
    pick = of_place(picks)
    for c, choice in enumerate(choices):

        @pl.when(pick == c)
        def _(choice=choice):
            turned[...] = choice[...].T

    side = 1 - lax.axis_index("context") % 2
    activate_heads(side, width, turned, slab, total, act_ref, state_ref)


def second_kernel(width, turned, slab, total, act_ref, state_ref):
    side = lax.axis_index("context") % 2
    activate_heads(side, width, turned, slab, total, act_ref, state_ref)


def activate(choices, picks, slab, total, heads, width):
    rows, tokens = choices[0].shape
    half = heads // 2
    columns = half * PARTS * width
    outs = (
        pltpu.VMEM((tokens, columns), BF16),
        pltpu.VMEM((half, width, width), F32),
    )
    cost = pl.CostEstimate(
        flops=2 * tokens * rows * columns + 2 * half * tokens * width * width,
        bytes_accessed=rows * tokens * 2,
        transcendentals=tokens * columns,
    )
    turned, act_other, state_other = pl.pallas_call(
        functools.partial(first_kernel, len(choices), width, picks),
        out_shape=(pltpu.VMEM((tokens, rows), BF16),) + outs,
        in_specs=[WHOLE] * (len(choices) + 2),
        out_specs=(WHOLE,) * 3,
        compiler_params=params(0),
        cost_estimate=cost,
        name="activate",
    )(*choices, slab, total)
    act_own, state_own = pl.pallas_call(
        functools.partial(second_kernel, width),
        out_shape=outs,
        in_specs=[WHOLE] * 3,
        out_specs=(WHOLE,) * 2,
        compiler_params=params(0),
        cost_estimate=cost,
        name="activate",
    )(turned, slab, total)
    return act_other, state_other, act_own, state_own


def within_kernel(width, *refs):
    tokens, columns = refs[0].shape
    causal = lax.broadcasted_iota(jnp.int32, (tokens, tokens), 0) >= lax.broadcasted_iota(
        jnp.int32, (tokens, tokens), 1
    )
    refs[4][...] = jnp.zeros_like(refs[4])
    for act_ref, within_ref in ((refs[0], refs[2]), (refs[1], refs[3])):
        for h in range(columns // (PARTS * width)):
            at = h * PARTS * width
            queries = act_ref[:, at : at + width]
            keys = act_ref[:, at + width : at + 2 * width]
            values = act_ref[:, at + 2 * width : at + 3 * width]
            scores = lax.dot_general(
                queries, keys, (((1,), (1,)), ((), ())), preferred_element_type=F32
            )
            scores = jnp.where(causal, scores, 0.0).astype(BF16)
            within_ref[:, h * width : (h + 1) * width] = jnp.dot(
                scores, values, preferred_element_type=F32
            )


def attend_within(act_other, act_own, width):
    tokens, columns = act_own.shape
    heads = columns // (PARTS * width)
    return pl.pallas_call(
        functools.partial(within_kernel, width),
        out_shape=(pltpu.VMEM((tokens, heads * width), F32),) * 2 + (pltpu.VMEM((8, 128), F32),),
        in_specs=[WHOLE] * 2,
        out_specs=(WHOLE,) * 3,
        compiler_params=params(0),
        cost_estimate=pl.CostEstimate(
            flops=8 * heads * tokens * tokens * width,
            bytes_accessed=tokens * columns * 4,
            transcendentals=0,
        ),
        name="within",
    )(act_other, act_own)


def across_kernel(own_side, n_groups, act, within, prior, *refs):
    groups = refs[:n_groups]
    *squares_in, att_ref, square_ref = refs[n_groups:]
    places = [(ref, h) for ref in groups for h in range(ref.shape[0])]
    half, width = len(places), prior.shape[1]
    core = lax.axis_index("context") % 2
    side = core if own_side else 1 - core
    squares = None
    for h, (earlier, place) in enumerate(places):
        carried = prior[side * half + h] + earlier[place]
        upper = carried.astype(BF16)
        lower = (carried - upper.astype(F32)).astype(BF16)
        at = h * PARTS * width
        queries = act[:, at : at + width]
        here = slice(h * width, (h + 1) * width)
        attended = within[:, here] + jnp.dot(
            jnp.concatenate([queries, queries], axis=1),
            jnp.concatenate([upper, lower], axis=0),
            preferred_element_type=F32,
        )
        att_ref[:, here] = attended
        square = attended * attended
        squares = square if squares is None else squares + square
    total = lax.dot_general(
        jnp.ones((8, width), F32),
        squares,
        (((1,), (1,)), ((), ())),
        preferred_element_type=F32,
        precision=lax.Precision.HIGHEST,
    )
    for ref in squares_in:
        total += ref[...]
    square_ref[...] = total


def attend_across(own_side, act, within, prior, earlier, squares):
    tokens = act.shape[0]
    half, width = prior.shape[0] // 2, prior.shape[1]
    operands = [act, within, prior] + earlier + squares
    return pl.pallas_call(
        functools.partial(across_kernel, own_side, len(earlier)),
        out_shape=(
            pltpu.VMEM((tokens, half * width), F32),
            pltpu.VMEM((8, tokens), F32),
        ),
        in_specs=[WHOLE] * len(operands),
        out_specs=(WHOLE, WHOLE),
        compiler_params=params(0),
        cost_estimate=pl.CostEstimate(
            flops=4 * half * tokens * width * width, bytes_accessed=0, transcendentals=0
        ),
        name="across",
    )(*operands)


def norm_kernel(features, att_other, att_own, gain_ref, *refs):
    *square_refs, out_ref, held, sems = refs
    core = lax.axis_index("context") % 2
    squares = sum(ref[...] for ref in square_refs[1:]) + square_refs[0][...]
    inverse = lax.rsqrt(squares[:1] * (1.0 / features) + EPSILON)
    inverse = jnp.broadcast_to(inverse, (128, squares.shape[1])).T
    columns = held.shape[2]
    parts = att_own.shape[1] // columns
    copies = []
    for side, att in ((1 - core, att_other), (core, att_own)):
        for part in range(parts):
            slot = len(copies)
            first = pl.multiple_of((side * parts + part) * columns, columns)
            for at in range(0, columns, 128):
                gain = gain_ref[:, pl.ds(pl.multiple_of(first + at, 128), 128)]
                here = slice(part * columns + at, part * columns + at + 128)
                held[slot, :, at : at + 128] = (att[:, here] * inverse * gain).astype(BF16)
            copies.append(
                pltpu.make_async_copy(
                    held.at[slot], out_ref.at[:, pl.ds(first, columns)], sems.at[slot]
                )
            )
            copies[-1].start()
    for copy in copies:
        copy.wait()


def normalize(att_other, att_own, squares, gain, features):
    tokens, half = att_own.shape
    columns = half // 2 if half % 256 == 0 else half
    count = 2 * half // columns
    return pl.pallas_call(
        functools.partial(norm_kernel, features),
        out_shape=jax.ShapeDtypeStruct((tokens, 2 * half), BF16),
        in_specs=[WHOLE] * (3 + len(squares)),
        out_specs=HBM,
        scratch_shapes=[
            pltpu.VMEM((count, tokens, columns), BF16),
            pltpu.SemaphoreType.DMA((count,)),
        ],
        compiler_params=params(4 * tokens * half),
        cost_estimate=pl.CostEstimate(
            flops=4 * tokens * half, bytes_accessed=4 * tokens * half, transcendentals=0
        ),
        name="normalize",
    )(att_other, att_own, gain[None, :], *squares)


def terms_over_tensor(x, n):
    if n & (n - 1):
        return [lax.psum(x, "tensor")]
    if n <= 4:
        return [x] + [
            lax.ppermute(x, "tensor", [(i, i ^ d) for i in range(n)]) for d in range(1, n)
        ]
    bit = 1
    while bit * 2 < n:
        x = x + lax.ppermute(x, "tensor", [(i, i ^ bit) for i in range(n)])
        bit *= 2
    return [x, lax.ppermute(x, "tensor", [(i, i ^ bit) for i in range(n)])]


def meet_kernel(bits, n_got, first, final, *refs):
    own, theirs, gots = refs[0], refs[1], refs[2 : 2 + n_got]
    index = lax.axis_index("context")
    core, chip = index % 2, index // 2
    rising = core == 0

    def has(bit):
        return chip // bit % 2 == 1

    for h in range(refs[-1].shape[0]):
        own_part, their_part = own[first + h], theirs[first + h]
        total = own_part + their_part
        reached = total
        before = jnp.zeros_like(total)
        for bit, ref in zip(bits, gots):
            got = ref[h].astype(F32)
            earlier = jnp.logical_or(core == 1, has(bit))
            before = before + jnp.where(earlier, got, 0.0)
            reached = reached + got
        if final:
            for_mate, mine = refs[-2:]
            for_mate[h] = before + jnp.where(rising, own_part, 0.0)
            mine[h] = before + jnp.where(rising, 0.0, their_part)
        else:
            falling = before + jnp.where(has(bits[-1 - n_got]), 0.0, total)
            refs[-1][h] = jnp.where(rising, reached, falling).astype(BF16)


def meet(bits, own, theirs, gots, after, first, count, final):
    _, width, _ = own.shape
    if final:
        out_shape = [pltpu.VMEM((count, width, width), F32)] * 2
    else:
        out_shape = [pltpu.VMEM((count, width, width), BF16)]
    operands = [own, theirs] + gots + after
    return pl.pallas_call(
        functools.partial(meet_kernel, bits, len(gots), first, final),
        out_shape=out_shape,
        in_specs=[WHOLE] * len(operands),
        out_specs=[WHOLE] * len(out_shape),
        compiler_params=params(0),
        cost_estimate=pl.CostEstimate(
            flops=4 * count * width * width, bytes_accessed=0, transcendentals=0
        ),
        name="meet",
    )(*operands)


def earlier_states(other_states, own, after, n):
    chips, half = n // 2, own.shape[0]
    swap = [(i, i ^ 1) for i in range(n)]
    theirs = lax.ppermute(other_states, "context", swap)
    bits = [1 << b for b in range((chips - 1).bit_length())]
    groups = [(0, half // 2), (half // 2, half - half // 2)]
    groups = [group for group in groups if group[1]]
    gots = [[] for _ in groups]
    for step, (rise, fall) in enumerate(zip(bits, bits[::-1])):
        pairs = [
            (2 * i + c, 2 * (i ^ bit) + c)
            for i in range(chips)
            for c, bit in enumerate((rise, fall))
        ]
        for g, group in enumerate(groups):
            waits = after if step == 1 and g == 0 else []
            (message,) = meet(bits, own, theirs, gots[g], waits, *group, False)
            gots[g] = gots[g] + [lax.ppermute(message, "context", pairs)]
    others, mine = [], []
    for g, group in enumerate(groups):
        for_mate, kept = meet(bits, own, theirs, gots[g], [], *group, True)
        others.append(lax.ppermute(for_mate, "context", swap))
        mine.append(kept)
    return others, mine


def hops(n):
    pairs = [[[] for _ in range(n - 1)] for _ in range(2)]
    arrivals = [[] for _ in range(n)]
    for t in range(n - 1):
        for chain in range(2):
            for share in range(n):
                way = 1 if share % 2 == chain else -1
                here = share + way * t
                if 0 <= here < n and 0 <= here + way < n:
                    pairs[chain][t].append((here, here + way))
                    if t == 1 and chain == 1:
                        pairs[chain][t].append((here + way, here))
                    arrivals[here + way].append((t, chain, share))
    pairs = [[sorted(set(p)) for p in chain] for chain in pairs]
    return pairs, arrivals


def body(n_tensor, n_context, tokens_t, qkv_weight, prior_state, norm_gain):
    share = tokens_t.shape[0]
    heads, width, _ = prior_state.shape
    early = share // 2

    pairs, arrivals = hops(n_tensor)
    last = n_tensor - 2
    pieces = cut_in_two(tokens_t, early)
    held = [[tokens_t], pieces]
    came = {}

    steps = [(-1, None), (0, None)] + [(1, 0), (1, 1)] + [(m, None) for m in range(2, last)]
    steps = [step for step in steps if step[0] < last] + [(last, 0)]

    def rows_of(m, piece):
        starts = [there[m][2] if m >= 0 else i for i, there in enumerate(arrivals)]
        return [start * share + (early if piece == 1 else 0) for start in starts]

    def count_of(piece):
        return {None: share, 0: early, 1: share - early}[piece]

    def run(number, ready, total, after):
        m, piece = steps[number]
        following = []
        if number + 1 < len(steps):
            following = [rows_of(*steps[number + 1]), count_of(steps[number + 1][1])]
            if number == 0:
                following += [rows_of(last, 1), share - early]
        choices, picks = [pieces], [0] * n_tensor
        if m >= 0:
            keys = sorted({there[m][:2] for there in arrivals})
            picks = [keys.index(there[m][:2]) for there in arrivals]
            choices = [came[key] if piece is None else [came[key][piece]] for key in keys]
        return project(
            choices, picks, qkv_weight, rows_of(m, piece), ready, total, after, *following
        )

    total, done, ready, slab = run(0, None, None, None)
    number = 1
    for t in range(n_tensor - 1):
        for chain in range(2):
            if pairs[chain][t]:
                held[chain] = [lax.ppermute(x, "tensor", pairs[chain][t]) for x in held[chain]]
                came[t, chain] = held[chain]
        if t == 0:
            if (0, 1) in came:
                held[1][0] = done = gate(held[1][0], done)
            held[0] = came[0, 0] = cut_in_two(held[0][0], early, [done])
            if (0, 1) in came:
                held[1][1] = gate(held[1][1], held[0][0])
        gates = [0, 1] if t == 1 and t < last else []
        while number < len(steps) - 1 and 1 <= t >= steps[number][0]:
            total, done, ready = run(number, ready, total, done)
            number += 1
            if gates:
                j = gates.pop(0)
                held[0][j] = done = gate(held[0][j], done)

    total, _ = run(number, ready, total, done)
    keys = sorted({there[last][:2] for there in arrivals})
    picks = [keys.index(there[last][:2]) for there in arrivals]
    choices = [came[key] for key in keys]
    other_act, other_states, own_act, own_states = activate(
        [c[1] for c in choices], picks, slab, total, heads, width
    )
    other_within, own_within, done = attend_within(other_act, own_act, width)
    other, own = earlier_states(other_states, own_states, [done], n_context)
    own_att, squares = attend_across(True, own_act, own_within, prior_state, own, [])
    other_att, squares = attend_across(
        False, other_act, other_within, prior_state, other, [squares]
    )
    squares = terms_over_tensor(squares, n_tensor)
    return normalize(other_att, own_att, squares, norm_gain, n_tensor * heads * width)


def solution(mesh):
    n_tensor, n_context = mesh.shape["tensor"], mesh.shape["context"]
    in_specs = (P("tensor", "context"), P(None, "tensor"), P("tensor", None, None), P("tensor"))
    return jax.shard_map(
        functools.partial(body, n_tensor, n_context),
        mesh=mesh,
        in_specs=in_specs,
        out_specs=P("context", "tensor"),
        check_vma=False,
    )
```

```python
import functools

import jax
import jax.numpy as jnp
from jax import lax
from jax.experimental import pallas as pl
from jax.experimental.pallas import tpu as pltpu
from jax.sharding import PartitionSpec as P

EPSILON = 1e-06
PARTS = 3
COLUMNS = 1024
SLOT_BYTES = 10 * 1024 * 1024
VMEM_EXTRA = 4 * 1024 * 1024

F32 = jnp.float32
BF16 = jnp.bfloat16


def params(scratch):
    return pltpu.CompilerParams(vmem_limit_bytes=scratch + VMEM_EXTRA)


HBM = pl.BlockSpec(memory_space=pltpu.HBM)
WHOLE = pl.BlockSpec(memory_space=pltpu.VMEM)
ANY = pl.BlockSpec(memory_space=pl.ANY)


def of_place(values):
    place = lax.axis_index("tensor")
    found = jnp.int32(values[0])
    for i, value in enumerate(values[1:], 1):
        if value != values[0]:
            found = jnp.where(place == i, jnp.int32(value), found)
    return found


def column_blocks(columns):
    width = COLUMNS if columns % COLUMNS == 0 else columns
    return [pl.ds(at, width) for at in range(0, columns, width)]


def turn_features(pick, choices, turned):
    for c, pieces in enumerate(choices):

        def turn(pieces=pieces):
            at = 0
            for piece in pieces:
                turned[:, at : at + piece.shape[0]] = piece[...].T
                at += piece.shape[0]

        if len(choices) == 1:
            turn()
        else:
            pl.when(pick == c)(turn)


def project_kernel(counts, first, picks, weight_rows, next_rows, slab_rows, *refs):
    refs = list(refs)
    choices = [[refs.pop(0) for _ in range(count)] for count in counts]
    weight = refs.pop(0)
    ready = None
    if not first:
        ready, _, _ = refs.pop(0), refs.pop(0), refs.pop(0)
    total, done = refs.pop(0), refs.pop(0)
    next_block = refs.pop(0) if next_rows else None
    slab = refs.pop(0) if slab_rows else None
    turned, held, weight_sems = refs
    done[...] = jnp.zeros_like(done)
    rows = turned.shape[1]
    slots = held.shape[0]
    blocks = column_blocks(weight.shape[1])

    at = pl.ds(pl.multiple_of(of_place(weight_rows), 16), rows)
    streamed = blocks if first else blocks[1:]
    copies = [
        pltpu.make_async_copy(weight.at[at, block], held.at[b % slots], weight_sems.at[b])
        for b, block in enumerate(streamed)
    ]
    if next_rows:
        at = pl.ds(pl.multiple_of(of_place(next_rows), 16), next_block.shape[0])
        copies.append(
            pltpu.make_async_copy(
                weight.at[at, blocks[0]], next_block, weight_sems.at[len(streamed)]
            )
        )
    if slab_rows:
        at = pl.ds(pl.multiple_of(of_place(slab_rows), 16), slab.shape[0])
        copies.append(
            pltpu.make_async_copy(weight.at[at, :], slab, weight_sems.at[len(copies)])
        )
    for copy in copies[:slots]:
        copy.start()
    turn_features(of_place(picks), choices, turned)
    for b, block in enumerate(blocks):
        b = b if first else b - 1
        if b < 0:
            matrix = ready[...]
        else:
            copies[b].wait()
            matrix = held[b % slots]
        product = jnp.dot(turned[...], matrix, preferred_element_type=F32)
        if first:
            total[:, block] = product
        else:
            total[:, block] += product
        if 0 <= b < len(copies) - slots:
            copies[b + slots].start()
    for copy in copies[len(streamed) :]:
        copy.wait()


def project(
    choices,
    picks,
    weight,
    weight_rows,
    ready,
    total,
    after,
    next_rows=None,
    next_count=0,
    slab_rows=None,
    slab_count=0,
):
    counts = [len(pieces) for pieces in choices]
    rows = sum(piece.shape[0] for piece in choices[0])
    tokens, columns = choices[0][0].shape[1], weight.shape[1]
    first = total is None
    flat = [piece for pieces in choices for piece in pieces]
    operands = flat + [weight] + ([] if first else [ready, after, total])
    blocks = column_blocks(columns)
    block = blocks[0].size
    slots = max(1, min(SLOT_BYTES // (2 * rows * block), len(blocks)))
    out_shape = [pltpu.VMEM((tokens, columns), F32), pltpu.VMEM((8, 128), F32)]
    if next_rows:
        out_shape.append(pltpu.VMEM((next_count, block), BF16))
    if slab_rows:
        out_shape.append(pltpu.VMEM((slab_count, columns), BF16))
    return pl.pallas_call(
        functools.partial(
            project_kernel, counts, first, picks, weight_rows, next_rows, slab_rows
        ),
        out_shape=out_shape,
        in_specs=[WHOLE] * len(flat) + [HBM] + ([] if first else [WHOLE, ANY, WHOLE]),
        out_specs=[WHOLE] * len(out_shape),
        scratch_shapes=[
            pltpu.VMEM((tokens, rows), BF16),
            pltpu.VMEM((slots, rows, block), BF16),
            pltpu.SemaphoreType.DMA((len(blocks) + 2,)),
        ],
        input_output_aliases={} if first else {len(operands) - 1: 0},
        compiler_params=params(2 * rows * (tokens + slots * block)),
        cost_estimate=pl.CostEstimate(
            flops=2 * tokens * rows * columns,
            bytes_accessed=rows * columns * 2 + rows * tokens * 2,
            transcendentals=0,
        ),
        name="project",
    )(*operands)


def gate_kernel(*refs):
    pass


def gate(x, after):
    return pl.pallas_call(
        gate_kernel,
        out_shape=jax.ShapeDtypeStruct(x.shape, x.dtype),
        in_specs=[ANY, ANY],
        out_specs=ANY,
        input_output_aliases={0: 0},
        compiler_params=params(0),
        name="gate",
    )(x, after)


def cut_kernel(x, *refs):
    *_, upper, lower, sems = refs
    rows = upper.shape[0]
    copies = [
        pltpu.make_async_copy(x.at[pl.ds(0, rows)], upper, sems.at[0]),
        pltpu.make_async_copy(x.at[pl.ds(rows, lower.shape[0])], lower, sems.at[1]),
    ]
    for copy in copies:
        copy.start()
    for copy in copies:
        copy.wait()


def cut_in_two(x, rows, after=()):
    sizes = (rows, x.shape[0] - rows)
    return list(
        pl.pallas_call(
            cut_kernel,
            out_shape=[pltpu.VMEM((size, x.shape[1]), x.dtype) for size in sizes],
            in_specs=[ANY if after else HBM] + [ANY] * len(after),
            out_specs=[WHOLE] * 2,
            scratch_shapes=[pltpu.SemaphoreType.DMA((2,))],
            compiler_params=params(0),
            name="cut",
        )(x, *after)
    )


def heads_at_once(half):
    return next(g for g in (4, 2, 1) if half % g == 0)


def activate_heads(side, width, turned, slab, total, act_ref, state_ref):
    half = state_ref.shape[0]
    group = PARTS * width
    at_once = heads_at_once(half)
    for h in range(0, half, at_once):
        here = slice(h * group, (h + at_once) * group)
        column = pl.multiple_of((side * half + h) * group, group)
        block = pl.ds(column, at_once * group)
        projected = total[:, block] + jnp.dot(
            turned[...],
            slab[slab.shape[0] - turned.shape[1] :, block],
            preferred_element_type=F32,
        )
        act = (projected / (1.0 + jnp.exp(-projected))).astype(BF16)
        act_ref[:, here] = act
        for g in range(at_once):
            at = g * group
            state_ref[h + g] = lax.dot_general(
                act[:, at + width : at + 2 * width],
                act[:, at + 2 * width : at + group],
                (((0,), (0,)), ((), ())),
                preferred_element_type=F32,
            )


def first_kernel(n_choices, width, picks, *refs):
    choices = refs[:n_choices]
    slab, total, turned, act_ref, state_ref = refs[n_choices:]
    turn_features(of_place(picks), [[choice] for choice in choices], turned)
    side = 1 - lax.axis_index("context") % 2
    activate_heads(side, width, turned, slab, total, act_ref, state_ref)


def second_kernel(width, turned, slab, total, act_ref, state_ref):
    side = lax.axis_index("context") % 2
    activate_heads(side, width, turned, slab, total, act_ref, state_ref)


def activate(choices, picks, slab, total, heads, width):
    rows, tokens = choices[0].shape
    half = heads // 2
    columns = half * PARTS * width
    outs = (
        pltpu.VMEM((tokens, columns), BF16),
        pltpu.VMEM((half, width, width), F32),
    )
    cost = pl.CostEstimate(
        flops=2 * tokens * rows * columns + 2 * half * tokens * width * width,
        bytes_accessed=rows * tokens * 2,
        transcendentals=tokens * columns,
    )
    turned, act_other, state_other = pl.pallas_call(
        functools.partial(first_kernel, len(choices), width, picks),
        out_shape=(pltpu.VMEM((tokens, rows), BF16),) + outs,
        in_specs=[WHOLE] * (len(choices) + 2),
        out_specs=(WHOLE,) * 3,
        compiler_params=params(0),
        cost_estimate=cost,
        name="activate",
    )(*choices, slab, total)
    act_own, state_own = pl.pallas_call(
        functools.partial(second_kernel, width),
        out_shape=outs,
        in_specs=[WHOLE] * 3,
        out_specs=(WHOLE,) * 2,
        compiler_params=params(0),
        cost_estimate=cost,
        name="activate",
    )(turned, slab, total)
    return act_other, state_other, act_own, state_own


def within_kernel(width, *refs):
    tokens, columns = refs[0].shape
    causal = lax.broadcasted_iota(jnp.int32, (tokens, tokens), 0) >= lax.broadcasted_iota(
        jnp.int32, (tokens, tokens), 1
    )
    refs[4][...] = jnp.zeros_like(refs[4])
    for act_ref, within_ref in ((refs[0], refs[2]), (refs[1], refs[3])):
        for h in range(columns // (PARTS * width)):
            at = h * PARTS * width
            queries = act_ref[:, at : at + width]
            keys = act_ref[:, at + width : at + 2 * width]
            values = act_ref[:, at + 2 * width : at + 3 * width]
            scores = lax.dot_general(
                queries, keys, (((1,), (1,)), ((), ())), preferred_element_type=F32
            )
            scores = jnp.where(causal, scores, 0.0).astype(BF16)
            within_ref[:, h * width : (h + 1) * width] = jnp.dot(
                scores, values, preferred_element_type=F32
            )


def attend_within(act_other, act_own, width):
    tokens, columns = act_own.shape
    heads = columns // (PARTS * width)
    return pl.pallas_call(
        functools.partial(within_kernel, width),
        out_shape=(pltpu.VMEM((tokens, heads * width), F32),) * 2 + (pltpu.VMEM((8, 128), F32),),
        in_specs=[WHOLE] * 2,
        out_specs=(WHOLE,) * 3,
        compiler_params=params(0),
        cost_estimate=pl.CostEstimate(
            flops=8 * heads * tokens * tokens * width,
            bytes_accessed=tokens * columns * 4,
            transcendentals=0,
        ),
        name="within",
    )(act_other, act_own)


def across_kernel(own_side, n_groups, act, within, prior, *refs):
    groups = refs[:n_groups]
    *squares_in, att_ref, square_ref = refs[n_groups:]
    places = [(ref, h) for ref in groups for h in range(ref.shape[0])]
    half, width = len(places), prior.shape[1]
    core = lax.axis_index("context") % 2
    side = core if own_side else 1 - core
    squares = None
    for h, (earlier, place) in enumerate(places):
        carried = prior[side * half + h] + earlier[place]
        upper = carried.astype(BF16)
        lower = (carried - upper.astype(F32)).astype(BF16)
        at = h * PARTS * width
        queries = act[:, at : at + width]
        here = slice(h * width, (h + 1) * width)
        attended = within[:, here] + jnp.dot(
            jnp.concatenate([queries, queries], axis=1),
            jnp.concatenate([upper, lower], axis=0),
            preferred_element_type=F32,
        )
        att_ref[:, here] = attended
        square = attended * attended
        squares = square if squares is None else squares + square
    total = lax.dot_general(
        jnp.ones((8, width), F32),
        squares,
        (((1,), (1,)), ((), ())),
        preferred_element_type=F32,
        precision=lax.Precision.HIGHEST,
    )
    for ref in squares_in:
        total += ref[...]
    square_ref[...] = total


def attend_across(own_side, act, within, prior, earlier, squares):
    tokens = act.shape[0]
    half, width = prior.shape[0] // 2, prior.shape[1]
    operands = [act, within, prior] + earlier + squares
    return pl.pallas_call(
        functools.partial(across_kernel, own_side, len(earlier)),
        out_shape=(
            pltpu.VMEM((tokens, half * width), F32),
            pltpu.VMEM((8, tokens), F32),
        ),
        in_specs=[WHOLE] * len(operands),
        out_specs=(WHOLE, WHOLE),
        compiler_params=params(0),
        cost_estimate=pl.CostEstimate(
            flops=4 * half * tokens * width * width, bytes_accessed=0, transcendentals=0
        ),
        name="across",
    )(*operands)


def norm_kernel(features, att_other, att_own, gain_ref, *refs):
    *square_refs, out_ref, held, sems = refs
    core = lax.axis_index("context") % 2
    squares = sum(ref[...] for ref in square_refs[1:]) + square_refs[0][...]
    inverse = lax.rsqrt(squares[:1] * (1.0 / features) + EPSILON)
    inverse = jnp.broadcast_to(inverse, (128, squares.shape[1])).T
    columns = held.shape[2]
    parts = att_own.shape[1] // columns
    copies = []
    for side, att in ((1 - core, att_other), (core, att_own)):
        for part in range(parts):
            slot = len(copies)
            first = pl.multiple_of((side * parts + part) * columns, columns)
            for at in range(0, columns, 128):
                gain = gain_ref[:, pl.ds(pl.multiple_of(first + at, 128), 128)]
                here = slice(part * columns + at, part * columns + at + 128)
                held[slot, :, at : at + 128] = (att[:, here] * inverse * gain).astype(BF16)
            copies.append(
                pltpu.make_async_copy(
                    held.at[slot], out_ref.at[:, pl.ds(first, columns)], sems.at[slot]
                )
            )
            copies[-1].start()
    for copy in copies:
        copy.wait()


def normalize(att_other, att_own, squares, gain, features):
    tokens, half = att_own.shape
    columns = half // 2 if half % 256 == 0 else half
    count = 2 * half // columns
    return pl.pallas_call(
        functools.partial(norm_kernel, features),
        out_shape=jax.ShapeDtypeStruct((tokens, 2 * half), BF16),
        in_specs=[WHOLE] * (3 + len(squares)),
        out_specs=HBM,
        scratch_shapes=[
            pltpu.VMEM((count, tokens, columns), BF16),
            pltpu.SemaphoreType.DMA((count,)),
        ],
        compiler_params=params(4 * tokens * half),
        cost_estimate=pl.CostEstimate(
            flops=4 * tokens * half, bytes_accessed=4 * tokens * half, transcendentals=0
        ),
        name="normalize",
    )(att_other, att_own, gain[None, :], *squares)


def terms_over_tensor(x, n):
    if n & (n - 1):
        return [lax.psum(x, "tensor")]
    if n <= 4:
        return [x] + [
            lax.ppermute(x, "tensor", [(i, i ^ d) for i in range(n)]) for d in range(n - 1, 0, -1)
        ]
    bit = 1
    while bit * 2 < n:
        x = x + lax.ppermute(x, "tensor", [(i, i ^ bit) for i in range(n)])
        bit *= 2
    return [x, lax.ppermute(x, "tensor", [(i, i ^ bit) for i in range(n)])]


def meet_kernel(bits, n_got, first, final, *refs):
    own, theirs, gots = refs[0], refs[1], refs[2 : 2 + n_got]
    index = lax.axis_index("context")
    core, chip = index % 2, index // 2
    rising = core == 0

    def has(bit):
        return chip // bit % 2 == 1

    for h in range(refs[-1].shape[0]):
        own_part, their_part = own[first + h], theirs[first + h]
        total = own_part + their_part
        reached = total
        before = jnp.zeros_like(total)
        for bit, ref in zip(bits, gots):
            got = ref[h].astype(F32)
            earlier = jnp.logical_or(core == 1, has(bit))
            before = before + jnp.where(earlier, got, 0.0)
            reached = reached + got
        if final:
            for_mate, mine = refs[-2:]
            for_mate[h] = before + jnp.where(rising, own_part, 0.0)
            mine[h] = before + jnp.where(rising, 0.0, their_part)
        else:
            falling = before + jnp.where(has(bits[-1 - n_got]), 0.0, total)
            refs[-1][h] = jnp.where(rising, reached, falling).astype(BF16)


def meet(bits, own, theirs, gots, after, first, count, final):
    _, width, _ = own.shape
    if final:
        out_shape = [pltpu.VMEM((count, width, width), F32)] * 2
    else:
        out_shape = [pltpu.VMEM((count, width, width), BF16)]
    operands = [own, theirs] + gots + after
    return pl.pallas_call(
        functools.partial(meet_kernel, bits, len(gots), first, final),
        out_shape=out_shape,
        in_specs=[WHOLE] * len(operands),
        out_specs=[WHOLE] * len(out_shape),
        compiler_params=params(0),
        cost_estimate=pl.CostEstimate(
            flops=4 * count * width * width, bytes_accessed=0, transcendentals=0
        ),
        name="meet",
    )(*operands)


def earlier_states(other_states, own, after, n):
    chips, half = n // 2, own.shape[0]
    swap = [(i, i ^ 1) for i in range(n)]
    theirs = lax.ppermute(other_states, "context", swap)
    bits = [1 << b for b in range((chips - 1).bit_length())]
    groups = [(0, half // 2), (half // 2, half - half // 2)]
    groups = [group for group in groups if group[1]]
    gots = [[] for _ in groups]
    for step, (rise, fall) in enumerate(zip(bits, bits[::-1])):
        pairs = [
            (2 * i + c, 2 * (i ^ bit) + c)
            for i in range(chips)
            for c, bit in enumerate((rise, fall))
        ]
        for g, group in enumerate(groups):
            waits = after if step == 1 and g == 0 else []
            (message,) = meet(bits, own, theirs, gots[g], waits, *group, False)
            gots[g] = gots[g] + [lax.ppermute(message, "context", pairs)]
    others, mine = [], []
    for g, group in enumerate(groups):
        for_mate, kept = meet(bits, own, theirs, gots[g], [], *group, True)
        others.append(lax.ppermute(for_mate, "context", swap))
        mine.append(kept)
    return others, mine


def hops(n):
    pairs = [[[] for _ in range(n - 1)] for _ in range(2)]
    arrivals = [[] for _ in range(n)]
    for t in range(n - 1):
        for chain in range(2):
            for share in range(n):
                way = 1 if share % 2 == chain else -1
                here = share + way * t
                if 0 <= here < n and 0 <= here + way < n:
                    pairs[chain][t].append((here, here + way))
                    arrivals[here + way].append((t, chain, share))
    pairs = [[sorted(set(p)) for p in chain] for chain in pairs]
    return pairs, arrivals


def body(n_tensor, n_context, tokens_t, qkv_weight, prior_state, norm_gain):
    share = tokens_t.shape[0]
    heads, width, _ = prior_state.shape
    early = share // 2

    pairs, arrivals = hops(n_tensor)
    last = n_tensor - 2
    pieces = cut_in_two(tokens_t, early)
    held = [[tokens_t], pieces]
    came = {}

    steps = [(-1, None), (0, None)] + [(1, 0), (1, 1)] + [(m, None) for m in range(2, last)]
    steps = [step for step in steps if step[0] < last] + [(last, 0)]
    slab_at = len(steps) - 2

    def rows_of(m, piece):
        starts = [there[m][2] if m >= 0 else i for i, there in enumerate(arrivals)]
        return [start * share + (early if piece == 1 else 0) for start in starts]

    def count_of(piece):
        return {None: share, 0: early, 1: share - early}[piece]

    def run(number, ready, total, after):
        m, piece = steps[number]
        following = []
        if number + 1 < len(steps):
            following = [rows_of(*steps[number + 1]), count_of(steps[number + 1][1])]
            if number == slab_at:
                following += [rows_of(last, 1), share - early]
        choices, picks = [pieces], [0] * n_tensor
        if m >= 0:
            keys = sorted({there[m][:2] for there in arrivals})
            picks = [keys.index(there[m][:2]) for there in arrivals]
            choices = [came[key] if piece is None else [came[key][piece]] for key in keys]
        return project(
            choices, picks, qkv_weight, rows_of(m, piece), ready, total, after, *following
        )

    total, done, ready, *slab = run(0, None, None, None)
    number = 1
    for t in range(n_tensor - 1):
        for chain in range(2):
            if pairs[chain][t]:
                held[chain] = [lax.ppermute(x, "tensor", pairs[chain][t]) for x in held[chain]]
                came[t, chain] = held[chain]
        if t == 0:
            if (0, 1) in came:
                held[1][0] = done = gate(held[1][0], done)
            held[0] = came[0, 0] = cut_in_two(held[0][0], early, [done])
            if (0, 1) in came:
                held[1][1] = gate(held[1][1], held[0][0])
        gates = [0, 1] if t == 1 and t < last else []
        while number < len(steps) - 1 and 1 <= t >= steps[number][0]:
            total, done, ready, *more = run(number, ready, total, done)
            slab += more
            number += 1
            if gates:
                j = gates.pop(0)
                held[0][j] = done = gate(held[0][j], done)

    total, _ = run(number, ready, total, done)
    keys = sorted({there[last][:2] for there in arrivals})
    picks = [keys.index(there[last][:2]) for there in arrivals]
    choices = [came[key] for key in keys]
    other_act, other_states, own_act, own_states = activate(
        [c[1] for c in choices], picks, slab[0], total, heads, width
    )
    other_within, own_within, done = attend_within(other_act, own_act, width)
    other, own = earlier_states(other_states, own_states, [done], n_context)
    own_att, squares = attend_across(True, own_act, own_within, prior_state, own, [])
    other_att, squares = attend_across(
        False, other_act, other_within, prior_state, other, [squares]
    )
    squares = terms_over_tensor(squares, n_tensor)
    return normalize(other_att, own_att, squares, norm_gain, n_tensor * heads * width)


def solution(mesh):
    n_tensor, n_context = mesh.shape["tensor"], mesh.shape["context"]
    in_specs = (P("tensor", "context"), P(None, "tensor"), P("tensor", None, None), P("tensor"))
    return jax.shard_map(
        functools.partial(body, n_tensor, n_context),
        mesh=mesh,
        in_specs=in_specs,
        out_specs=P("context", "tensor"),
        check_vma=False,
    )
```

```python
import functools

import jax
import jax.numpy as jnp
from jax import lax
from jax.experimental import pallas as pl
from jax.experimental.pallas import tpu as pltpu
from jax.sharding import PartitionSpec as P

EPSILON = 1e-06
PARTS = 3
COLUMNS = 1024
SLOT_BYTES = 10 * 1024 * 1024
VMEM_EXTRA = 4 * 1024 * 1024

F32 = jnp.float32
BF16 = jnp.bfloat16


def params(scratch):
    return pltpu.CompilerParams(vmem_limit_bytes=scratch + VMEM_EXTRA)


HBM = pl.BlockSpec(memory_space=pltpu.HBM)
WHOLE = pl.BlockSpec(memory_space=pltpu.VMEM)
ANY = pl.BlockSpec(memory_space=pl.ANY)


def of_place(values):
    place = lax.axis_index("tensor")
    found = jnp.int32(values[0])
    for i, value in enumerate(values[1:], 1):
        if value != values[0]:
            found = jnp.where(place == i, jnp.int32(value), found)
    return found


def column_blocks(columns):
    width = COLUMNS if columns % COLUMNS == 0 else columns
    return [pl.ds(at, width) for at in range(0, columns, width)]


def turn_features(pick, choices, turned):
    for c, pieces in enumerate(choices):

        def turn(pieces=pieces):
            at = 0
            for piece in pieces:
                turned[:, at : at + piece.shape[0]] = piece[...].T
                at += piece.shape[0]

        if len(choices) == 1:
            turn()
        else:
            pl.when(pick == c)(turn)


def project_kernel(counts, first, picks, weight_rows, next_rows, slab_rows, *refs):
    refs = list(refs)
    choices = [[refs.pop(0) for _ in range(count)] for count in counts]
    weight = refs.pop(0)
    ready = None
    if not first:
        ready, _, _ = refs.pop(0), refs.pop(0), refs.pop(0)
    total, done = refs.pop(0), refs.pop(0)
    next_block = refs.pop(0) if next_rows else None
    slab = refs.pop(0) if slab_rows else None
    turned, held, weight_sems = refs
    done[...] = jnp.zeros_like(done)
    rows = turned.shape[1]
    slots = held.shape[0]
    blocks = column_blocks(weight.shape[1])

    at = pl.ds(pl.multiple_of(of_place(weight_rows), 16), rows)
    streamed = blocks if first else blocks[1:]
    copies = [
        pltpu.make_async_copy(weight.at[at, block], held.at[b % slots], weight_sems.at[b])
        for b, block in enumerate(streamed)
    ]
    if next_rows:
        at = pl.ds(pl.multiple_of(of_place(next_rows), 16), next_block.shape[0])
        copies.append(
            pltpu.make_async_copy(
                weight.at[at, blocks[0]], next_block, weight_sems.at[len(streamed)]
            )
        )
    if slab_rows:
        at = pl.ds(pl.multiple_of(of_place(slab_rows), 16), slab.shape[0])
        copies.append(
            pltpu.make_async_copy(weight.at[at, :], slab, weight_sems.at[len(copies)])
        )
    for copy in copies[:slots]:
        copy.start()
    turn_features(of_place(picks), choices, turned)
    for b, block in enumerate(blocks):
        b = b if first else b - 1
        if b < 0:
            matrix = ready[...]
        else:
            copies[b].wait()
            matrix = held[b % slots]
        product = jnp.dot(turned[...], matrix, preferred_element_type=F32)
        if first:
            total[:, block] = product
        else:
            total[:, block] += product
        if 0 <= b < len(copies) - slots:
            copies[b + slots].start()
    for copy in copies[len(streamed) :]:
        copy.wait()


def project(
    choices,
    picks,
    weight,
    weight_rows,
    ready,
    total,
    after,
    next_rows=None,
    next_count=0,
    slab_rows=None,
    slab_count=0,
):
    counts = [len(pieces) for pieces in choices]
    rows = sum(piece.shape[0] for piece in choices[0])
    tokens, columns = choices[0][0].shape[1], weight.shape[1]
    first = total is None
    flat = [piece for pieces in choices for piece in pieces]
    operands = flat + [weight] + ([] if first else [ready, after, total])
    blocks = column_blocks(columns)
    block = blocks[0].size
    slots = max(1, min(SLOT_BYTES // (2 * rows * block), len(blocks)))
    out_shape = [pltpu.VMEM((tokens, columns), F32), pltpu.VMEM((8, 128), F32)]
    if next_rows:
        out_shape.append(pltpu.VMEM((next_count, block), BF16))
    if slab_rows:
        out_shape.append(pltpu.VMEM((slab_count, columns), BF16))
    return pl.pallas_call(
        functools.partial(
            project_kernel, counts, first, picks, weight_rows, next_rows, slab_rows
        ),
        out_shape=out_shape,
        in_specs=[WHOLE] * len(flat) + [HBM] + ([] if first else [WHOLE, ANY, WHOLE]),
        out_specs=[WHOLE] * len(out_shape),
        scratch_shapes=[
            pltpu.VMEM((tokens, rows), BF16),
            pltpu.VMEM((slots, rows, block), BF16),
            pltpu.SemaphoreType.DMA((len(blocks) + 2,)),
        ],
        input_output_aliases={} if first else {len(operands) - 1: 0},
        compiler_params=params(2 * rows * (tokens + slots * block)),
        cost_estimate=pl.CostEstimate(
            flops=2 * tokens * rows * columns,
            bytes_accessed=rows * columns * 2 + rows * tokens * 2,
            transcendentals=0,
        ),
        name="project",
    )(*operands)


def gate_kernel(*refs):
    pass


def gate(x, after):
    return pl.pallas_call(
        gate_kernel,
        out_shape=jax.ShapeDtypeStruct(x.shape, x.dtype),
        in_specs=[ANY, ANY],
        out_specs=ANY,
        input_output_aliases={0: 0},
        compiler_params=params(0),
        name="gate",
    )(x, after)


def cut_kernel(x, *refs):
    *_, upper, lower, sems = refs
    rows = upper.shape[0]
    copies = [
        pltpu.make_async_copy(x.at[pl.ds(0, rows)], upper, sems.at[0]),
        pltpu.make_async_copy(x.at[pl.ds(rows, lower.shape[0])], lower, sems.at[1]),
    ]
    for copy in copies:
        copy.start()
    for copy in copies:
        copy.wait()


def cut_in_two(x, rows, after=()):
    sizes = (rows, x.shape[0] - rows)
    return list(
        pl.pallas_call(
            cut_kernel,
            out_shape=[pltpu.VMEM((size, x.shape[1]), x.dtype) for size in sizes],
            in_specs=[ANY if after else HBM] + [ANY] * len(after),
            out_specs=[WHOLE] * 2,
            scratch_shapes=[pltpu.SemaphoreType.DMA((2,))],
            compiler_params=params(0),
            name="cut",
        )(x, *after)
    )


def heads_at_once(half):
    return next(g for g in (4, 2, 1) if half % g == 0)


def activate_heads(side, width, turned, slab, total, act_ref, state_ref):
    half = state_ref.shape[0]
    group = PARTS * width
    at_once = heads_at_once(half)
    for h in range(0, half, at_once):
        here = slice(h * group, (h + at_once) * group)
        column = pl.multiple_of((side * half + h) * group, group)
        block = pl.ds(column, at_once * group)
        projected = total[:, block] + jnp.dot(
            turned[...],
            slab[slab.shape[0] - turned.shape[1] :, block],
            preferred_element_type=F32,
        )
        act = (projected / (1.0 + jnp.exp(-projected))).astype(BF16)
        act_ref[:, here] = act
        for g in range(at_once):
            at = g * group
            state_ref[h + g] = lax.dot_general(
                act[:, at + width : at + 2 * width],
                act[:, at + 2 * width : at + group],
                (((0,), (0,)), ((), ())),
                preferred_element_type=F32,
            )


def first_kernel(n_choices, width, picks, *refs):
    choices = refs[:n_choices]
    slab, total, turned, act_ref, state_ref = refs[n_choices:]
    turn_features(of_place(picks), [[choice] for choice in choices], turned)
    side = 1 - lax.axis_index("context") % 2
    activate_heads(side, width, turned, slab, total, act_ref, state_ref)


def second_kernel(width, turned, slab, total, act_ref, state_ref):
    side = lax.axis_index("context") % 2
    activate_heads(side, width, turned, slab, total, act_ref, state_ref)


def activate(choices, picks, slab, total, heads, width):
    rows, tokens = choices[0].shape
    half = heads // 2
    columns = half * PARTS * width
    outs = (
        pltpu.VMEM((tokens, columns), BF16),
        pltpu.VMEM((half, width, width), F32),
    )
    cost = pl.CostEstimate(
        flops=2 * tokens * rows * columns + 2 * half * tokens * width * width,
        bytes_accessed=rows * tokens * 2,
        transcendentals=tokens * columns,
    )
    turned, act_other, state_other = pl.pallas_call(
        functools.partial(first_kernel, len(choices), width, picks),
        out_shape=(pltpu.VMEM((tokens, rows), BF16),) + outs,
        in_specs=[WHOLE] * (len(choices) + 2),
        out_specs=(WHOLE,) * 3,
        compiler_params=params(0),
        cost_estimate=cost,
        name="activate",
    )(*choices, slab, total)
    act_own, state_own = pl.pallas_call(
        functools.partial(second_kernel, width),
        out_shape=outs,
        in_specs=[WHOLE] * 3,
        out_specs=(WHOLE,) * 2,
        compiler_params=params(0),
        cost_estimate=cost,
        name="activate",
    )(turned, slab, total)
    return act_other, state_other, act_own, state_own


def within_kernel(width, *refs):
    tokens, columns = refs[0].shape
    causal = lax.broadcasted_iota(jnp.int32, (tokens, tokens), 0) >= lax.broadcasted_iota(
        jnp.int32, (tokens, tokens), 1
    )
    refs[4][...] = jnp.zeros_like(refs[4])
    for act_ref, within_ref in ((refs[0], refs[2]), (refs[1], refs[3])):
        for h in range(columns // (PARTS * width)):
            at = h * PARTS * width
            queries = act_ref[:, at : at + width]
            keys = act_ref[:, at + width : at + 2 * width]
            values = act_ref[:, at + 2 * width : at + 3 * width]
            scores = lax.dot_general(
                queries, keys, (((1,), (1,)), ((), ())), preferred_element_type=F32
            )
            scores = jnp.where(causal, scores, 0.0).astype(BF16)
            within_ref[:, h * width : (h + 1) * width] = jnp.dot(
                scores, values, preferred_element_type=F32
            )


def attend_within(act_other, act_own, width):
    tokens, columns = act_own.shape
    heads = columns // (PARTS * width)
    return pl.pallas_call(
        functools.partial(within_kernel, width),
        out_shape=(pltpu.VMEM((tokens, heads * width), F32),) * 2 + (pltpu.VMEM((8, 128), F32),),
        in_specs=[WHOLE] * 2,
        out_specs=(WHOLE,) * 3,
        compiler_params=params(0),
        cost_estimate=pl.CostEstimate(
            flops=8 * heads * tokens * tokens * width,
            bytes_accessed=tokens * columns * 4,
            transcendentals=0,
        ),
        name="within",
    )(act_other, act_own)


def across_kernel(own_side, n_groups, act, within, prior, *refs):
    groups = refs[:n_groups]
    *squares_in, att_ref, square_ref = refs[n_groups:]
    places = [(ref, h) for ref in groups for h in range(ref.shape[0])]
    half, width = len(places), prior.shape[1]
    core = lax.axis_index("context") % 2
    side = core if own_side else 1 - core
    squares = None
    for h, (earlier, place) in enumerate(places):
        carried = prior[side * half + h] + earlier[place]
        upper = carried.astype(BF16)
        lower = (carried - upper.astype(F32)).astype(BF16)
        at = h * PARTS * width
        queries = act[:, at : at + width]
        here = slice(h * width, (h + 1) * width)
        attended = within[:, here] + jnp.dot(
            jnp.concatenate([queries, queries], axis=1),
            jnp.concatenate([upper, lower], axis=0),
            preferred_element_type=F32,
        )
        att_ref[:, here] = attended
        square = attended * attended
        squares = square if squares is None else squares + square
    total = lax.dot_general(
        jnp.ones((8, width), F32),
        squares,
        (((1,), (1,)), ((), ())),
        preferred_element_type=F32,
        precision=lax.Precision.HIGHEST,
    )
    for ref in squares_in:
        total += ref[...]
    square_ref[...] = total


def attend_across(own_side, act, within, prior, earlier, squares):
    tokens = act.shape[0]
    half, width = prior.shape[0] // 2, prior.shape[1]
    operands = [act, within, prior] + earlier + squares
    return pl.pallas_call(
        functools.partial(across_kernel, own_side, len(earlier)),
        out_shape=(
            pltpu.VMEM((tokens, half * width), F32),
            pltpu.VMEM((8, tokens), F32),
        ),
        in_specs=[WHOLE] * len(operands),
        out_specs=(WHOLE, WHOLE),
        compiler_params=params(0),
        cost_estimate=pl.CostEstimate(
            flops=4 * half * tokens * width * width, bytes_accessed=0, transcendentals=0
        ),
        name="across",
    )(*operands)


def norm_kernel(features, att_other, att_own, gain_ref, *refs):
    *square_refs, out_ref, held, sems = refs
    core = lax.axis_index("context") % 2
    squares = sum(ref[...] for ref in square_refs[1:]) + square_refs[0][...]
    inverse = lax.rsqrt(squares[:1] * (1.0 / features) + EPSILON)
    inverse = jnp.broadcast_to(inverse, (128, squares.shape[1])).T
    columns = held.shape[2]
    parts = att_own.shape[1] // columns
    copies = []
    for side, att in ((1 - core, att_other), (core, att_own)):
        for part in range(parts):
            slot = len(copies)
            first = pl.multiple_of((side * parts + part) * columns, columns)
            for at in range(0, columns, 128):
                gain = gain_ref[:, pl.ds(pl.multiple_of(first + at, 128), 128)]
                here = slice(part * columns + at, part * columns + at + 128)
                held[slot, :, at : at + 128] = (att[:, here] * inverse * gain).astype(BF16)
            copies.append(
                pltpu.make_async_copy(
                    held.at[slot], out_ref.at[:, pl.ds(first, columns)], sems.at[slot]
                )
            )
            copies[-1].start()
    for copy in copies:
        copy.wait()


def normalize(att_other, att_own, squares, gain, features):
    tokens, half = att_own.shape
    columns = half // 2 if half % 256 == 0 else half
    count = 2 * half // columns
    return pl.pallas_call(
        functools.partial(norm_kernel, features),
        out_shape=jax.ShapeDtypeStruct((tokens, 2 * half), BF16),
        in_specs=[WHOLE] * (3 + len(squares)),
        out_specs=HBM,
        scratch_shapes=[
            pltpu.VMEM((count, tokens, columns), BF16),
            pltpu.SemaphoreType.DMA((count,)),
        ],
        compiler_params=params(4 * tokens * half),
        cost_estimate=pl.CostEstimate(
            flops=4 * tokens * half, bytes_accessed=4 * tokens * half, transcendentals=0
        ),
        name="normalize",
    )(att_other, att_own, gain[None, :], *squares)


def terms_over_tensor(x, n):
    if n & (n - 1):
        return [lax.psum(x, "tensor")]
    if n <= 4:
        return [x] + [
            lax.ppermute(x, "tensor", [(i, i ^ d) for i in range(n)]) for d in range(n - 1, 0, -1)
        ]
    bit = 1
    while bit * 2 < n:
        x = x + lax.ppermute(x, "tensor", [(i, i ^ bit) for i in range(n)])
        bit *= 2
    return [x, lax.ppermute(x, "tensor", [(i, i ^ bit) for i in range(n)])]


def meet_kernel(bits, n_got, first, final, *refs):
    own, theirs, gots = refs[0], refs[1], refs[2 : 2 + n_got]
    index = lax.axis_index("context")
    core, chip = index % 2, index // 2
    rising = core == 0

    def has(bit):
        return chip // bit % 2 == 1

    for h in range(refs[-1].shape[0]):
        own_part, their_part = own[first + h], theirs[first + h]
        total = own_part + their_part
        reached = total
        before = jnp.zeros_like(total)
        for bit, ref in zip(bits, gots):
            got = ref[h].astype(F32)
            earlier = jnp.logical_or(core == 1, has(bit))
            before = before + jnp.where(earlier, got, 0.0)
            reached = reached + got
        if final:
            for_mate, mine = refs[-2:]
            for_mate[h] = before + jnp.where(rising, own_part, 0.0)
            mine[h] = before + jnp.where(rising, 0.0, their_part)
        else:
            falling = before + jnp.where(has(bits[-1 - n_got]), 0.0, total)
            refs[-1][h] = jnp.where(rising, reached, falling).astype(BF16)


def meet(bits, own, theirs, gots, after, first, count, final):
    _, width, _ = own.shape
    if final:
        out_shape = [pltpu.VMEM((count, width, width), F32)] * 2
    else:
        out_shape = [pltpu.VMEM((count, width, width), BF16)]
    operands = [own, theirs] + gots + after
    return pl.pallas_call(
        functools.partial(meet_kernel, bits, len(gots), first, final),
        out_shape=out_shape,
        in_specs=[WHOLE] * len(operands),
        out_specs=[WHOLE] * len(out_shape),
        compiler_params=params(0),
        cost_estimate=pl.CostEstimate(
            flops=4 * count * width * width, bytes_accessed=0, transcendentals=0
        ),
        name="meet",
    )(*operands)


def earlier_states(other_states, own, after, n):
    chips, half = n // 2, own.shape[0]
    swap = [(i, i ^ 1) for i in range(n)]
    theirs = lax.ppermute(other_states, "context", swap)
    bits = [1 << b for b in range((chips - 1).bit_length())]
    groups = [(0, half // 2), (half // 2, half - half // 2)]
    groups = [group for group in groups if group[1]]
    gots = [[] for _ in groups]
    for step, (rise, fall) in enumerate(zip(bits, bits[::-1])):
        pairs = [
            (2 * i + c, 2 * (i ^ bit) + c)
            for i in range(chips)
            for c, bit in enumerate((rise, fall))
        ]
        for g, group in enumerate(groups):
            waits = after if step == 1 and g == 0 else []
            (message,) = meet(bits, own, theirs, gots[g], waits, *group, False)
            gots[g] = gots[g] + [lax.ppermute(message, "context", pairs)]
    others, mine = [], []
    for g, group in enumerate(groups):
        for_mate, kept = meet(bits, own, theirs, gots[g], [], *group, True)
        others.append(lax.ppermute(for_mate, "context", swap))
        mine.append(kept)
    return others, mine


def hops(n):
    pairs = [[[] for _ in range(n - 1)] for _ in range(2)]
    arrivals = [[] for _ in range(n)]
    for t in range(n - 1):
        for chain in range(2):
            for share in range(n):
                way = 1 if share % 2 == chain else -1
                here = share + way * t
                if 0 <= here < n and 0 <= here + way < n:
                    pairs[chain][t].append((here, here + way))
                    arrivals[here + way].append((t, chain, share))
    pairs = [[sorted(set(p)) for p in chain] for chain in pairs]
    return pairs, arrivals


def body(n_tensor, n_context, tokens_t, qkv_weight, prior_state, norm_gain):
    share = tokens_t.shape[0]
    heads, width, _ = prior_state.shape
    early = share // 2

    pairs, arrivals = hops(n_tensor)
    last = n_tensor - 2
    pieces = [tokens_t[:early], tokens_t[early:]]
    held = [[tokens_t], pieces]
    came = {}

    steps = [(-1, None), (0, None)] + [(1, 0), (1, 1)] + [(m, None) for m in range(2, last)]
    steps = [step for step in steps if step[0] < last] + [(last, 0)]
    slab_at = len(steps) - 2

    def rows_of(m, piece):
        starts = [there[m][2] if m >= 0 else i for i, there in enumerate(arrivals)]
        return [start * share + (early if piece == 1 else 0) for start in starts]

    def count_of(piece):
        return {None: share, 0: early, 1: share - early}[piece]

    def run(number, ready, total, after):
        m, piece = steps[number]
        following = []
        if number + 1 < len(steps):
            following = [rows_of(*steps[number + 1]), count_of(steps[number + 1][1])]
            if number == slab_at:
                following += [rows_of(last, 1), share - early]
        choices, picks = [pieces], [0] * n_tensor
        if m >= 0:
            keys = sorted({there[m][:2] for there in arrivals})
            picks = [keys.index(there[m][:2]) for there in arrivals]
            choices = [came[key] if piece is None else [came[key][piece]] for key in keys]
        return project(
            choices, picks, qkv_weight, rows_of(m, piece), ready, total, after, *following
        )

    total, done, ready, *slab = run(0, None, None, None)
    number = 1
    for t in range(n_tensor - 1):
        for chain in range(2):
            if pairs[chain][t]:
                held[chain] = [lax.ppermute(x, "tensor", pairs[chain][t]) for x in held[chain]]
                came[t, chain] = held[chain]
        if t == 0:
            if (0, 1) in came:
                held[1][0] = done = gate(held[1][0], done)
            held[0] = came[0, 0] = cut_in_two(held[0][0], early, [done])
            if (0, 1) in came:
                held[1][1] = gate(held[1][1], held[0][0])
        gates = [0, 1] if t == 1 and t < last else []
        while number < len(steps) - 1 and 1 <= t >= steps[number][0]:
            total, done, ready, *more = run(number, ready, total, done)
            slab += more
            number += 1
            if gates:
                j = gates.pop(0)
                held[0][j] = done = gate(held[0][j], done)

    total, _ = run(number, ready, total, done)
    keys = sorted({there[last][:2] for there in arrivals})
    picks = [keys.index(there[last][:2]) for there in arrivals]
    choices = [came[key] for key in keys]
    other_act, other_states, own_act, own_states = activate(
        [c[1] for c in choices], picks, slab[0], total, heads, width
    )
    other_within, own_within, done = attend_within(other_act, own_act, width)
    other, own = earlier_states(other_states, own_states, [done], n_context)
    own_att, squares = attend_across(True, own_act, own_within, prior_state, own, [])
    other_att, squares = attend_across(
        False, other_act, other_within, prior_state, other, [squares]
    )
    squares = terms_over_tensor(squares, n_tensor)
    return normalize(other_att, own_att, squares, norm_gain, n_tensor * heads * width)


def solution(mesh):
    n_tensor, n_context = mesh.shape["tensor"], mesh.shape["context"]
    in_specs = (P("tensor", "context"), P(None, "tensor"), P("tensor", None, None), P("tensor"))
    return jax.shard_map(
        functools.partial(body, n_tensor, n_context),
        mesh=mesh,
        in_specs=in_specs,
        out_specs=P("context", "tensor"),
        check_vma=False,
    )
```
